32 devices in a mesh: row: 8 (over y, x, core), col: 4 (over z).
Axes of the slice: x: 2, y: 2, z: 4, core: 2. Of those that a mesh axis runs over, the one named last changes fastest.
Arguments:
- z_trunk: bfloat16 [512, 512, 128], P('row', 'col'), may hold values from -6 to 6
- coords: int32 [3, 512], P(None, ('row', 'col')), may hold values from 0 to 255
- token_mask: int32 [512], P(('row', 'col')), may hold values 0 or 1
- w_dist: bfloat16 [39, 128], replicated, may hold values from -6 to 6
- w_attn: bfloat16 [128, 512], replicated, may hold values from -0.5 to 0.5
- w_bias: bfloat16 [128, 4], replicated, may hold values from -100 to 100
- w_out: bfloat16 [128, 128], replicated, may hold values from -2 to 2
- w_pae: bfloat16 [128, 64], replicated, may hold values from -0.5 to 0.5
- w_pde: bfloat16 [128, 64], replicated, may hold values from -0.5 to 0.5
Outputs:
- logits: float32 [512, 512, 128], P('row', 'col')
The draws below stay inside these ranges and needn't reach their ends.
All inputs are finite; a program needn't handle non-finite values. No bound on the sum of `token_mask` on one device may be relied on, other than what follows from the above.
Results may differ from the reference program's by a relative error of at most 0.0055.
The reference program's roundings to bfloat16 on the way count: a program that leaves them out, or rounds other values in their place, can miss the bound.
Values may be sent and summed in bfloat16 or wider, within the bound.
No kernel may reach another device: no remote copies, remote signals or barrier semaphores. Data moves between devices by JAX's collectives and lax.ppermute only.
A program may use at most 192 MiB of HBM per device.

```python
import jax
import jax.numpy as jnp
from jax import lax

C = 128
H = 4
BINS = 64
DBINS = 39
N = 512


def draw_w_bias(key, part):
    base = jax.random.normal(jax.random.fold_in(key, 11), (C, H), jnp.float32)
    order = jax.random.permutation(jax.random.fold_in(key, 12), H).astype(jnp.float32)
    levels = 0.6 * 2.0 ** (0.5 * order)
    scaled = base * levels[None, :] * C ** (-0.5)
    return jnp.clip(scaled, -100.0, 100.0).astype(jnp.bfloat16)


def place_ends(drawn, own_key, low, largest):
    index_at = [jax.random.randint(jax.random.fold_in(own_key, axis), (), 0, length) for axis, length in enumerate(drawn.shape)]
    longest = drawn.shape.index(max(drawn.shape))
    beside = index_at[:longest] + [(index_at[longest] + 1) % drawn.shape[longest]] + index_at[longest + 1:]
    return drawn.at[tuple(index_at)].set(low).at[tuple(beside)].set(largest)


def level_of(stream_key, shape, split, smallest, high):
    gain, own = 1.0, jax.random.fold_in(stream_key, 6)
    for dim, parts in split:
        draws = jnp.exp(jax.random.uniform(jax.random.fold_in(own, dim), (parts,), jnp.float32, smallest / len(split), high / len(split)))
        gain = gain * jnp.repeat(draws, shape[dim] // parts).reshape([-1 if axis == dim else 1 for axis in range(len(shape))])
    return gain


def bell_draw(own_key, dims, spread, most, cuts=(), held_as=jnp.bfloat16):
    array = jax.random.normal(own_key, dims, jnp.float32) * spread
    if len(cuts) > 0:
        array = level_of(own_key, dims, cuts, -0.22, 0.18) * array
    return jnp.clip(array, min=-most, max=most).astype(held_as)


def setup_inputs(seed: int = 0) -> dict:
    splits = jax.random.split(jax.random.key(seed), 10)
    return {
        "z_trunk": bell_draw(splits[0], (N, N, C), 1.0, 6.0, ((0, 8), (1, 4))),
        "coords": place_ends(jax.random.randint(splits[1], (3, N), 0, 256), jax.random.fold_in(splits[1], 1), 0, 255).astype(jnp.int32),
        "token_mask": place_ends((jax.random.randint(splits[2], (N,), 0, 8) < 7).astype(jnp.int32), jax.random.fold_in(splits[2], 1), 0, 1),
        "w_dist": bell_draw(splits[3], (DBINS, C), 1.0, 6.0),
        "w_attn": bell_draw(splits[4], (C, 4 * C), C ** -0.5, 0.5),
        "w_bias": draw_w_bias(jax.random.fold_in(splits[9], 71), 0),
        "w_out": bell_draw(splits[6], (C, C), 0.35, 2.0),
        "w_pae": bell_draw(splits[7], (C, BINS), C ** -0.5, 0.5),
        "w_pde": bell_draw(splits[8], (C, BINS), C ** -0.5, 0.5),
    }


def layer_norm(values):
    widened = values.astype(jnp.float32)
    average = lax.optimization_barrier(jnp.mean(widened, axis=-1, keepdims=True))
    centred = widened - average
    variance = lax.optimization_barrier(jnp.mean(centred * centred, axis=-1, keepdims=True))
    return (centred * lax.rsqrt(variance + 1e-05)).astype(jnp.bfloat16)

def distance_bins(coord_rows, coord_cols, class_count):
    offsets = coord_rows[:, :, None] - coord_cols[:, None, :]
    squared = lax.optimization_barrier(jnp.sum(offsets * offsets, axis=0))
    bin_edges = 27 + 4 * jnp.arange(class_count - 1, dtype=jnp.int32)
    above = (squared[:, :, None] > (bin_edges * bin_edges)[None, None, :]).astype(jnp.int32)
    return lax.optimization_barrier(jnp.sum(above, axis=-1))

def attend_column(query_rows, key_rows, value_rows, bias_full, key_bias):
    length_all = query_rows.shape[0]
    block_rows = min(512, length_all)

    def one_block(first_row):
        query_block = lax.dynamic_slice_in_dim(query_rows, first_row, block_rows, 0).astype(jnp.float32)
        bias_block = lax.dynamic_slice_in_dim(bias_full, first_row, block_rows, 2)
        scores = jnp.einsum('khd,ihd->hki', key_rows.astype(jnp.float32), query_block)
        scores = scores + bias_block + key_bias[None, :, None]
        highest = lax.optimization_barrier(jnp.max(scores, axis=1, keepdims=True))
        raised = jnp.exp(scores - highest)
        weights = (raised / lax.optimization_barrier(jnp.sum(raised, axis=1, keepdims=True))).astype(jnp.bfloat16)
        return jnp.einsum('hki,khd->ihd', weights.astype(jnp.float32), value_rows.astype(jnp.float32))
    starts = jnp.arange(length_all // block_rows, dtype=jnp.int32) * block_rows
    blocks_out = lax.map(one_block, starts)
    return blocks_out.reshape(length_all, query_rows.shape[1], query_rows.shape[2])

def reference(z_trunk, coords, token_mask, w_dist, w_attn, w_bias, w_out, w_pae, w_pde):
    total = z_trunk.shape[0]
    width = z_trunk.shape[2]
    heads = w_bias.shape[1]
    head_dim = width // heads
    bins_all = distance_bins(coords, coords, w_dist.shape[0])
    pair = (z_trunk.astype(jnp.float32) + w_dist.astype(jnp.float32)[bins_all]).astype(jnp.bfloat16)
    normed = layer_norm(pair)
    bias_flat = jnp.dot(normed.reshape(-1, width), w_bias, preferred_element_type=jnp.float32)
    bias_full = bias_flat.reshape(total, total, heads).transpose(2, 0, 1)
    key_bias = (token_mask.astype(jnp.float32) - 1.0) * 30000.0

    def one_column(operands):
        normed_col, pair_col = operands
        projected = jnp.dot(normed_col, w_attn, preferred_element_type=jnp.float32)
        query_rows = (projected[:, :width] * head_dim ** (-0.5)).astype(jnp.bfloat16).reshape(total, heads, head_dim)
        key_rows = projected[:, width:2 * width].astype(jnp.bfloat16).reshape(total, heads, head_dim)
        value_rows = projected[:, 2 * width:3 * width].astype(jnp.bfloat16).reshape(total, heads, head_dim)
        gate_rows = projected[:, 3 * width:].astype(jnp.bfloat16)
        attended = attend_column(query_rows, key_rows, value_rows, bias_full, key_bias).reshape(total, width)
        gated = (jax.nn.sigmoid(gate_rows.astype(jnp.float32)) * attended).astype(jnp.bfloat16)
        update = jnp.dot(gated, w_out, preferred_element_type=jnp.float32)
        return (pair_col.astype(jnp.float32) + update).astype(jnp.bfloat16)
    updated_swapped = lax.map(one_column, (jnp.swapaxes(normed, 0, 1), jnp.swapaxes(pair, 0, 1)))
    updated = jnp.swapaxes(updated_swapped, 0, 1)
    symmetric = updated.astype(jnp.float32) + jnp.swapaxes(updated, 0, 1).astype(jnp.float32)
    pae_part = jnp.dot(layer_norm(updated).reshape(-1, width), w_pae, preferred_element_type=jnp.float32)
    pde_part = jnp.dot(layer_norm(symmetric).reshape(-1, width), w_pde, preferred_element_type=jnp.float32)
    return jnp.concatenate([pae_part, pde_part], axis=1).reshape(total, total, -1)
```

```python
import functools

import jax
import jax.numpy as jnp
from jax import lax
from jax.experimental import pallas as pl
from jax.experimental.pallas import tpu as pltpu
from jax.sharding import PartitionSpec as P

F32 = jnp.float32
BF16 = jnp.bfloat16
NT = (((1,), (1,)), ((), ()))
VMEM_LIMIT = 56 * 1024 * 1024


def normalise(values):
    average = jnp.mean(values, axis=-1, keepdims=True)
    centred = values - average
    variance = jnp.mean(centred * centred, axis=-1, keepdims=True)
    return (centred * lax.rsqrt(variance + 1e-05)).astype(BF16)


def pair_kernel(classes, slab, batch, row_coords, col_coords, low, high, z, w_dist, w_bias, pair, bias, wide, spread):
    rows_dev, cols_dev, width = z.shape
    heads = bias.shape[0]
    for axis in range(3):
        line = jnp.broadcast_to(col_coords[axis : axis + 1, :], (width, cols_dev))
        spread[axis] = jnp.transpose(line)

    def some_rows(step, carry):
        first = step * batch
        hots = []
        for at in range(batch):
            squared = jnp.zeros((cols_dev, width), F32)
            for axis in range(3):
                offset = spread[axis] - row_coords[axis, first + at].astype(F32)
                squared = squared + offset * offset
            inside = (squared > low[...]) & (squared <= high[...])
            hots.append(jnp.where(inside, 1.0, 0.0).astype(BF16))
        embedded = jnp.dot(jnp.concatenate(hots, axis=0), w_dist[...], preferred_element_type=F32)
        values = z[pl.ds(first, batch)].reshape(batch * cols_dev, width).astype(F32)
        rounded = (values + embedded).astype(BF16).astype(F32)
        wide[pl.ds(first * cols_dev, batch * cols_dev), :] = rounded
        normed = normalise(rounded)
        found = lax.dot_general(w_bias[...], normed, NT, preferred_element_type=F32)
        for at in range(batch):
            for head in range(heads):
                bias[head, pl.ds(first + at, 1), :] = found[head : head + 1, at * cols_dev : (at + 1) * cols_dev]
        return carry

    lax.fori_loop(0, rows_dev // batch, some_rows, 0)

    def some_cols(step, carry):
        for at in range(slab):
            column = wide[pl.ds(step * slab + at, rows_dev, stride=cols_dev), :]
            pair[step, at] = column.astype(BF16)
        return carry

    lax.fori_loop(0, cols_dev // slab, some_cols, 0)


def attention_kernel(heads, chunk, pair, bias, key_bias, w_key, w_rest, w_out, updated, biased):
    n_rows, _, rows_dev, width = pair.shape
    n_cols = bias.shape[1]
    cols_dev = bias.shape[4]
    total = n_rows * rows_dev
    head_dim = width // heads

    @pl.when(pl.program_id(0) == 0)
    def _():
        for head in range(heads):
            for block in range(n_cols):
                biased[head, :, block * cols_dev : (block + 1) * cols_dev] = (
                    bias[:, block, head].reshape(total, cols_dev) + key_bias[...]
                )

    values = pair[:, 0].reshape(total, width).astype(F32)
    normed = normalise(values)
    key = jnp.dot(normed, w_key[...], preferred_element_type=F32).astype(BF16)
    rest = lax.dot_general(w_rest[...], normed, NT, preferred_element_type=F32)
    query = (rest[:width] * head_dim ** (-0.5)).astype(BF16)
    value = rest[width : 2 * width].astype(BF16)
    gate = jax.nn.sigmoid(rest[2 * width :].astype(BF16).astype(F32))
    ones = jnp.ones((16, total), BF16)
    parts = []
    for head in range(heads):
        lo, hi = head * head_dim, (head + 1) * head_dim
        pieces = []
        if lo:
            pieces.append(jnp.zeros((lo, total), BF16))
        pieces.append(query[lo:hi])
        if hi < width:
            pieces.append(jnp.zeros((width - hi, total), BF16))
        own_query = jnp.concatenate(pieces, axis=0)
        own_value = jnp.concatenate([value[lo:hi], ones], axis=0)
        lanes = []
        for first in range(0, total, chunk):
            score = jnp.dot(key, own_query[:, first : first + chunk], preferred_element_type=F32)
            score = score + biased[head, :, first : first + chunk]
            highest = jnp.max(score, axis=0, keepdims=True)
            raised = jnp.exp(score - highest).astype(BF16)
            summed = jnp.dot(own_value, raised, preferred_element_type=F32)
            lanes.append(summed[:head_dim] / summed[head_dim : head_dim + 1])
        parts.append(jnp.concatenate(lanes, axis=1))
    attended = jnp.concatenate(parts, axis=0)
    gated = (gate * attended).astype(BF16)
    update = jnp.dot(w_out[...], gated, preferred_element_type=F32)
    result = (values + jnp.transpose(update)).astype(BF16)
    updated[:, 0] = result.reshape(n_rows, rows_dev, width)


def logits_kernel(spots, own, mirrored, w_both, logits, wide):
    slab = mirrored.shape[2]
    rows_dev, width = mirrored.shape[3], mirrored.shape[4]
    cols_dev = logits.shape[1]
    pieces = cols_dev // rows_dev
    block = pl.program_id(0)

    @pl.when(block == 0)
    def _():
        wide[...] = own[...].reshape(cols_dev * rows_dev, width).astype(F32)

    first = spots[block] * slab
    for at in range(slab):
        mine = wide[pl.ds(first + at, cols_dev, stride=rows_dev), :]
        other = mirrored[0, :, at].reshape(cols_dev, width).astype(F32)
        both = jnp.concatenate([normalise(mine), normalise(mine + other)], axis=1)
        logits[at] = jnp.dot(both, w_both[...], preferred_element_type=F32)


def per_device(z_trunk, coords, token_mask, w_dist, w_attn, w_bias, w_out, w_pae, w_pde):
    rows_dev, cols_dev, width = z_trunk.shape
    n_rows, n_cols = lax.axis_size("row"), lax.axis_size("col")
    devices = n_rows * n_cols
    total = rows_dev * n_rows
    slab = rows_dev // n_cols
    heads = w_bias.shape[1]
    classes = w_dist.shape[0]
    share = coords.shape[1]
    both_axes = ("row", "col")
    row_at, col_at = lax.axis_index("row"), lax.axis_index("col")

    tokens = jnp.concatenate([coords, token_mask[None, :]], axis=0)
    copies = jnp.broadcast_to(tokens[None], (devices,) + tokens.shape)
    spread = lax.all_to_all(copies, both_axes, split_axis=0, concat_axis=0, tiled=True)
    tokens = spread.transpose(1, 0, 2).reshape(4, total)
    row_coords = lax.dynamic_slice_in_dim(tokens, row_at * rows_dev, rows_dev, 1)
    col_coords = lax.dynamic_slice_in_dim(tokens, col_at * cols_dev, cols_dev, 1).astype(F32)
    key_bias = jnp.broadcast_to(
        ((tokens[3].astype(F32) - 1.0) * 30000.0)[:, None], (total, cols_dev)
    )

    edges = (27.0 + 4.0 * jnp.arange(classes - 1, dtype=F32)) ** 2
    low = jnp.concatenate([jnp.full((1,), -1.0, F32), edges, jnp.full((width - classes,), 1e9, F32)])
    high = jnp.concatenate([edges, jnp.full((width - classes + 1,), 1e9, F32)])
    w_dist_full = jnp.pad(w_dist, ((0, width - classes), (0, 0)))
    w_bias_t = jnp.pad(w_bias.T, ((0, 16 - heads), (0, 0)))

    vmem = pl.BlockSpec(memory_space=pltpu.VMEM)
    smem = pl.BlockSpec(memory_space=pltpu.SMEM)
    pair, bias = pl.pallas_call(
        functools.partial(pair_kernel, classes, slab, 4),
        out_shape=(
            jax.ShapeDtypeStruct((n_rows, slab, rows_dev, width), BF16),
            jax.ShapeDtypeStruct((heads, rows_dev, cols_dev), F32),
        ),
        in_specs=[smem] + [vmem] * 6,
        out_specs=(vmem, vmem),
        scratch_shapes=[
            pltpu.VMEM((rows_dev * cols_dev, width), F32),
            pltpu.VMEM((3, cols_dev, width), F32),
        ],
        compiler_params=pltpu.CompilerParams(vmem_limit_bytes=VMEM_LIMIT),
        name="pair_kernel",
    )(row_coords, col_coords, low[None], high[None], z_trunk, w_dist_full, w_bias_t)

    bias = lax.all_gather(bias, "col", axis=0, tiled=False)
    bias = lax.all_gather(bias, "row", axis=0, tiled=False)
    pair = lax.all_to_all(pair, "row", split_axis=0, concat_axis=0, tiled=True)

    w_key = w_attn[:, width : 2 * width]
    w_rest = jnp.concatenate(
        [w_attn[:, :width], w_attn[:, 2 * width : 3 * width], w_attn[:, 3 * width :]], axis=1
    ).T
    whole = lambda shape: pl.BlockSpec(shape, lambda j: (0,) * len(shape))
    column = pl.BlockSpec((n_rows, 1, rows_dev, width), lambda j: (0, j, 0, 0))
    updated = pl.pallas_call(
        functools.partial(attention_kernel, heads, 2 * cols_dev),
        out_shape=jax.ShapeDtypeStruct(pair.shape, BF16),
        grid=(slab,),
        in_specs=[
            column,
            whole(bias.shape),
            whole(key_bias.shape),
            whole(w_key.shape),
            whole(w_rest.shape),
            whole(w_out.shape),
        ],
        out_specs=column,
        scratch_shapes=[pltpu.VMEM((heads, total, total), F32)],
        compiler_params=pltpu.CompilerParams(vmem_limit_bytes=VMEM_LIMIT),
        name="attention_kernel",
    )(pair, bias, key_bias, w_key, w_rest, w_out.T)

    per_tile = n_rows // n_cols
    got = []
    for shift in range(n_cols):
        hops = []
        for r in range(n_rows):
            for c in range(n_cols):
                to = (per_tile * c + r // n_cols) * n_cols + (r % n_cols + shift) % n_cols
                hops.append((r * n_cols + c, to))
        part = lax.dynamic_slice_in_dim(
            updated, per_tile * ((row_at % n_cols + shift) % n_cols), per_tile, 0
        )
        got.append(lax.ppermute(part, both_axes, hops))
    mirrored = jnp.stack(got)
    spots = (col_at - jnp.arange(n_cols, dtype=jnp.int32)) % n_cols
    own = lax.all_to_all(updated, "row", split_axis=0, concat_axis=0, tiled=True)

    bins = w_pae.shape[1]
    w_both = jnp.concatenate(
        [jnp.pad(w_pae, ((0, 0), (0, bins))), jnp.pad(w_pde, ((0, 0), (bins, 0)))], axis=0
    )
    logits = pl.pallas_call(
        logits_kernel,
        out_shape=jax.ShapeDtypeStruct((rows_dev, cols_dev, 2 * bins), F32),
        grid_spec=pltpu.PrefetchScalarGridSpec(
            num_scalar_prefetch=1,
            grid=(n_cols,),
            in_specs=[
                pl.BlockSpec(own.shape, lambda b, at: (0, 0, 0, 0)),
                pl.BlockSpec((1,) + mirrored.shape[1:], lambda b, at: (b, 0, 0, 0, 0)),
                pl.BlockSpec(w_both.shape, lambda b, at: (0, 0)),
            ],
            out_specs=pl.BlockSpec((slab, cols_dev, 2 * bins), lambda b, at: (at[b], 0, 0)),
            scratch_shapes=[pltpu.VMEM((cols_dev * rows_dev, width), F32)],
        ),
        compiler_params=pltpu.CompilerParams(vmem_limit_bytes=VMEM_LIMIT),
        name="logits_kernel",
    )(spots, own, mirrored, w_both)
    return logits


def solution(mesh):
    in_specs = (
        P("row", "col", None),
        P(None, ("row", "col")),
        P(("row", "col")),
        P(),
        P(),
        P(),
        P(),
        P(),
        P(),
    )
    out_specs = P("row", "col", None)
    return jax.shard_map(
        per_device, mesh=mesh, in_specs=in_specs, out_specs=out_specs, check_vma=False
    )
```

```python
import functools

import jax
import jax.numpy as jnp
from jax import lax
from jax.experimental import pallas as pl
from jax.experimental.pallas import tpu as pltpu
from jax.sharding import PartitionSpec as P

F32 = jnp.float32
BF16 = jnp.bfloat16
NT = (((1,), (1,)), ((), ()))
VMEM_LIMIT = 56 * 1024 * 1024
AXES = ("row", "col")


def means(parts):
    width = parts[0].shape[-1]
    stacked = jnp.concatenate(parts, axis=1) if len(parts) > 1 else parts[0]
    return jnp.dot(stacked, jnp.full((stacked.shape[1], width), 1.0 / width, BF16), preferred_element_type=F32)


def normalise(values, parts):
    centred = values - means(parts)
    squares = centred * centred
    high = squares.astype(BF16)
    variance = means([high, (squares - high.astype(F32)).astype(BF16)])
    return (centred * lax.rsqrt(variance + 1e-05)).astype(BF16)


def embed(squares, low, high, w_dist, values):
    hots = []
    for squared in squares:
        inside = (squared > low[...]) & (squared <= high[...])
        hots.append(jnp.where(inside, 1.0, 0.0).astype(BF16))
    hot = jnp.concatenate(hots, axis=0) if len(hots) > 1 else hots[0]
    embedded = jnp.dot(hot, w_dist[...], preferred_element_type=F32)
    return (values + embedded).astype(BF16)


def squared_distance(spread, scalars, token):
    squared = None
    for axis in range(3):
        offset = spread[axis] - scalars[axis, token].astype(F32)
        squared = offset * offset if squared is None else squared + offset * offset
    return squared


def spread_lines(lines, spread):
    length, width = spread.shape[1:]
    for axis in range(3):
        for first in range(0, length, width):
            line = lines[axis : axis + 1, first : first + width].astype(F32)
            spread[axis, first : first + width] = jnp.transpose(jnp.broadcast_to(line, (width, width)))


def bias_kernel(batch, scalars, tokens, low, high, z, w_dist, w_bias, bias, found, spread):
    rows_dev, cols_dev, width = z.shape
    heads = found.shape[0]
    row_at, col_at = lax.axis_index("row"), lax.axis_index("col")
    spread_lines(tokens[:, pl.ds(pl.multiple_of(col_at * cols_dev, cols_dev), cols_dev)], spread)

    def some_rows(step, carry):
        first = step * batch
        values = z[pl.ds(first, batch)].reshape(batch * cols_dev, width).astype(F32)
        squares = [squared_distance(spread, scalars, row_at * rows_dev + first + at) for at in range(batch)]
        pair = embed(squares, low, high, w_dist, values)
        normed = normalise(pair.astype(F32), [pair])
        lines = lax.dot_general(w_bias[...], normed, NT, preferred_element_type=F32)
        for at in range(batch):
            for head in range(heads):
                found[head, pl.ds(first + at, 1), :] = lines[head : head + 1, at * cols_dev : (at + 1) * cols_dev]
        return carry

    lax.fori_loop(0, rows_dev // batch, some_rows, 0)
    swap = row_at % 2 == 1
    for duo in range(heads // 2):
        even, odd = found[2 * duo], found[2 * duo + 1]
        lines = jnp.concatenate([jnp.where(swap, odd, even), jnp.where(swap, even, odd)], axis=0)
        bias[duo] = jnp.transpose(lines)


def project_kernel(
    head_dim, batch, scalars, tokens, low, high, z, w_dist, w_key, w_rest, pair, key, query, value, gate, wide, spread
):
    total, slab, width = z.shape
    row_at, col_at = lax.axis_index("row"), lax.axis_index("col")
    cols_dev = spread.shape[2]
    half = cols_dev // 2

    @pl.when(pl.program_id(0) == 0)
    def _():
        spread_lines(tokens, spread)
        wide[...] = z[...].reshape(total * slab, width).astype(F32)

    first = pl.program_id(0) * batch
    own = col_at * cols_dev + row_at * slab + first
    values = jnp.concatenate([wide[pl.ds(first + at, total, stride=slab), :] for at in range(batch)], axis=0)
    squares = [squared_distance(spread, scalars, own + at) for at in range(batch)]
    rounded = embed(squares, low, high, w_dist, values)
    normed = normalise(rounded.astype(F32), [rounded])
    rest = jnp.dot(normed, w_rest[...], preferred_element_type=F32)
    odd_lane = lax.broadcasted_iota(jnp.int32, (1, width), 1) // head_dim % 2 == 1
    odd_row = lax.broadcasted_iota(jnp.int32, (width, 1), 0) // head_dim % 2 == 1
    for at in range(batch):
        rows = slice(at * total, (at + 1) * total)
        pair[at] = rounded[rows]
        query[at] = (rest[rows, :width] * head_dim ** (-0.5)).astype(BF16)
        gate[at] = rest[rows, 2 * width :].astype(BF16)
        values = rest[rows, width : 2 * width]
        swapped = []
        for start in range(0, total, 2 * half):
            swapped += [values[start + half : start + 2 * half], values[start : start + half]]
        value[at] = jnp.where(odd_lane, jnp.concatenate(swapped, axis=0), values).astype(BF16)
        lines = lax.dot_general(w_key[...], normed[rows], NT, preferred_element_type=F32)
        for start in range(0, total, 2 * half):
            block = lines[:, start : start + 2 * half]
            key[at, :, start : start + 2 * half] = jnp.where(odd_row, pltpu.roll(block, half, 1), block).astype(BF16)


def attention_kernel(heads, n_rows, tokens, key, query, value, gate, pair, w_out, *refs):
    bias = refs[:n_rows]
    updated, mirrored, biased, result = refs[n_rows], refs[n_rows + 1 : -2], refs[-2], refs[-1]
    width, total = key.shape[1:]
    n_cols, _, cols_dev, _ = bias[0].shape
    rows_dev = updated.shape[2]
    halves = n_rows // n_cols
    head_dim = width // heads
    row_at, col_at = lax.axis_index("row"), lax.axis_index("col")
    lane = lax.broadcasted_iota(jnp.int32, (1, width), 1)

    @pl.when(pl.program_id(0) == 0)
    def _():
        from_own = (lane < rows_dev) != (row_at % 2 == 1)
        for step in range(0, n_rows, 2):
            spot = (row_at ^ step) // 2
            start = pl.multiple_of(spot * cols_dev, cols_dev)
            mask = (tokens[3:4, pl.ds(start, cols_dev)].astype(F32) - 1.0) * 30000.0
            for duo in range(heads // 2):
                masks = [mask, jnp.concatenate([mask[:, rows_dev:], mask[:, :rows_dev]], axis=1)]
                for block in range(n_cols):
                    tiles = bias[step][block, duo], bias[step + 1][block, duo]
                    rows = pl.ds(pl.multiple_of((col_at ^ block) * cols_dev, cols_dev), cols_dev)
                    biased[spot, 2 * duo, rows] = jnp.where(from_own, tiles[0], tiles[1]) + masks[0]
                    biased[spot, 2 * duo + 1, rows] = jnp.where(from_own, tiles[1], tiles[0]) + masks[1]

    own_key, own_query = key[0], query[0]
    own_value = jnp.concatenate([value[0], jnp.ones((total, width), BF16)], axis=1)
    attended = jnp.zeros((total, width), F32)
    for head in range(heads):
        inside = lane // head_dim == head
        score = jnp.dot(jnp.where(inside, own_query, jnp.zeros((), BF16)), own_key, preferred_element_type=F32)
        score = score + jnp.concatenate([biased[spot, head] for spot in range(biased.shape[0])], axis=1)
        highest = jnp.max(score, axis=1, keepdims=True)
        raised = jnp.exp(score - highest).astype(BF16)
        summed = jnp.dot(raised, own_value, preferred_element_type=F32)
        attended = jnp.where(inside, summed[:, :width] / summed[:, width:], attended)
    gated = (jax.nn.sigmoid(gate[0].astype(F32)) * attended).astype(BF16)
    update = jnp.dot(gated, w_out[...], preferred_element_type=F32)
    result[...] = (pair[0].astype(F32) + update).astype(BF16).reshape(result.shape)
    updated[:, 0] = result[...]
    for shift in range(n_cols):
        block = (row_at % n_cols) ^ shift
        mirrored[shift][:, 0] = result[pl.ds(block * halves, halves)]


def logits_kernel(n_cols, rounds, *refs):
    own = refs[1 : 1 + rounds]
    mirrored = refs[1 + rounds : 1 + rounds + rounds * n_cols]
    w_both, logits, wide = refs[1 + rounds + rounds * n_cols :]
    n_rows, part, rows_dev, width = own[0].shape
    halves = n_rows // n_cols
    cols_dev = halves * rows_dev
    slab = rounds * part
    at_shift = pl.program_id(0)

    @pl.when(at_shift == 0)
    def _():
        size = part * rows_dev
        for row in range(n_rows):
            for step in range(rounds):
                first = (row * rounds + step) * size
                wide[first : first + size, :] = own[step][row].reshape(size, width).astype(F32)

    first = refs[0][at_shift] * slab
    for shift in range(n_cols):

        @pl.when(at_shift == shift)
        def _():
            for step in range(rounds):
                mine, other = [], []
                for at in range(part):
                    mine.append(wide[pl.ds(first + step * part + at, cols_dev, stride=rows_dev), :])
                    other += [mirrored[step * n_cols + shift][half, at] for half in range(halves)]
                mine, other = jnp.concatenate(mine, axis=0), jnp.concatenate(other, axis=0)
                mine_short = mine.astype(BF16)
                both = jnp.concatenate(
                    [normalise(mine, [mine_short]), normalise(mine + other.astype(F32), [mine_short, other])], axis=1
                )
                found = jnp.dot(both, w_both[...], preferred_element_type=F32)
                logits[step * part : (step + 1) * part] = found.reshape(part, cols_dev, found.shape[1])


def swap_over(array, axis, step, count):
    return lax.ppermute(array, axis, [(at, at ^ step) for at in range(count)])


def per_device(z_trunk, coords, token_mask, w_dist, w_attn, w_bias, w_out, w_pae, w_pde):
    rows_dev, cols_dev, width = z_trunk.shape
    n_rows, n_cols = lax.axis_size("row"), lax.axis_size("col")
    devices = n_rows * n_cols
    total = rows_dev * n_rows
    slab = rows_dev // n_cols
    halves = cols_dev // rows_dev
    heads = w_bias.shape[1]
    head_dim = width // heads
    classes = w_dist.shape[0]
    row_at, col_at = lax.axis_index("row"), lax.axis_index("col")
    params = pltpu.CompilerParams(vmem_limit_bytes=VMEM_LIMIT)
    vmem = pl.BlockSpec(memory_space=pltpu.VMEM)
    smem = pl.BlockSpec(memory_space=pltpu.SMEM)
    once = pl.Buffered(1)
    whole = lambda array: pl.BlockSpec(array.shape, lambda *at: (0,) * array.ndim, pipeline_mode=once)

    edges = (27.0 + 4.0 * jnp.arange(classes - 1, dtype=F32)) ** 2
    low = jnp.concatenate([jnp.full((1,), -1.0, F32), edges, jnp.full((width - classes,), 1e9, F32)])[None]
    high = jnp.concatenate([edges, jnp.full((width - classes + 1,), 1e9, F32)])[None]
    w_dist_full = jnp.pad(w_dist, ((0, width - classes), (0, 0)))
    w_bias_t = jnp.pad(w_bias.T, ((0, 16 - heads), (0, 0)))

    tokens = jnp.concatenate([coords, token_mask[None, :]], axis=0)
    copies = jnp.broadcast_to(tokens[None], (devices,) + tokens.shape)
    tokens = lax.all_to_all(copies, AXES, split_axis=0, concat_axis=0, tiled=True)
    tokens = tokens.transpose(1, 0, 2).reshape(4, total)
    z_parts = z_trunk.reshape(rows_dev, n_rows, slab, width).swapaxes(0, 1)
    z_parts, w_dist_full, w_bias_t = lax.optimization_barrier((z_parts, w_dist_full, w_bias_t))
    z_cols = lax.all_to_all(z_parts, "row", split_axis=0, concat_axis=0, tiled=True)
    z_cols = z_cols.reshape(total, slab, width)

    bias = pl.pallas_call(
        functools.partial(bias_kernel, 16),
        out_shape=jax.ShapeDtypeStruct((heads // 2, cols_dev, 2 * rows_dev), F32),
        in_specs=[smem] + [vmem] * 6,
        out_specs=vmem,
        scratch_shapes=[pltpu.VMEM((heads, rows_dev, cols_dev), F32), pltpu.VMEM((3, cols_dev, width), F32)],
        compiler_params=params,
        cost_estimate=pl.CostEstimate(flops=rows_dev * cols_dev * width * 300, bytes_accessed=1 << 22, transcendentals=0),
        name="bias_kernel",
    )(tokens, tokens, low, high, z_trunk, w_dist_full, w_bias_t)

    plane = jnp.stack([bias] + [swap_over(bias, "col", step, n_cols) for step in range(1, n_cols)])
    plane, z_cols = lax.optimization_barrier((plane, z_cols))
    held = {0: plane}
    for step in range(2, n_rows, 2):
        held[step] = swap_over(plane, "row", step, n_rows)

    w_key = w_attn[:, width : 2 * width].T
    w_rest = jnp.concatenate([w_attn[:, :width], w_attn[:, 2 * width :]], axis=1)
    batch = 4
    by_rows = pl.BlockSpec((batch, total, width), lambda j: (j, 0, 0))
    by_lanes = pl.BlockSpec((batch, width, total), lambda j: (j, 0, 0))
    rows_shape = jax.ShapeDtypeStruct((slab, total, width), BF16)
    lanes_shape = jax.ShapeDtypeStruct((slab, width, total), BF16)
    projected = pl.pallas_call(
        functools.partial(project_kernel, head_dim, batch),
        out_shape=(rows_shape, lanes_shape, rows_shape, rows_shape, rows_shape),
        grid=(slab // batch,),
        in_specs=[smem, whole(tokens), vmem, vmem, whole(z_cols), vmem, vmem, vmem],
        out_specs=(by_rows, by_lanes, by_rows, by_rows, by_rows),
        scratch_shapes=[pltpu.VMEM((total * slab, width), F32), pltpu.VMEM((3, total, width), F32)],
        compiler_params=params,
        cost_estimate=pl.CostEstimate(flops=total * slab * width * 2000, bytes_accessed=1 << 24, transcendentals=0),
        name="project_kernel",
    )(tokens, tokens, low, high, z_cols, w_dist_full, w_key, w_rest)
    far = [held[step] for step in range(2, n_rows, 2)]
    far, projected = lax.optimization_barrier((far, projected))
    for step, tile in zip(range(2, n_rows, 2), far):
        held[step] = tile
    for step in range(0, n_rows, 2):
        held[step + 1] = swap_over(held[step], "row", 1, n_rows)
    pair, key, query, value, gate = projected

    rounds = 2
    part = slab // rounds
    own, mirrored = [], []
    for step in range(rounds):
        rows_spec = pl.BlockSpec((1, total, width), lambda j, step=step: (j + step * part, 0, 0))
        lanes_spec = pl.BlockSpec((1, width, total), lambda j, step=step: (j + step * part, 0, 0))
        out_spec = lambda count: pl.BlockSpec((count, 1, rows_dev, width), lambda j: (0, j, 0, 0))
        out_shape = lambda count: jax.ShapeDtypeStruct((count, part, rows_dev, width), BF16)
        updated, *turned = pl.pallas_call(
            functools.partial(attention_kernel, heads, n_rows),
            out_shape=(out_shape(n_rows),) + (out_shape(halves),) * n_cols,
            grid=(part,),
            in_specs=[whole(tokens), lanes_spec, rows_spec, rows_spec, rows_spec, rows_spec, whole(w_out)]
            + [whole(plane)] * n_rows,
            out_specs=(out_spec(n_rows),) + (out_spec(halves),) * n_cols,
            scratch_shapes=[
                pltpu.VMEM((total // cols_dev, heads, total, cols_dev), F32),
                pltpu.VMEM((n_rows, rows_dev, width), BF16),
            ],
            compiler_params=params,
            cost_estimate=pl.CostEstimate(
                flops=4 * part * total * total * heads * 256,
                bytes_accessed=1 << 24,
                transcendentals=part * heads * total * total,
            ),
            name="attention_kernel",
        )(tokens, key, query, value, gate, pair, w_out, *[held[at] for at in range(n_rows)])
        if step:
            updated, turned, own, mirrored = lax.optimization_barrier((updated, turned, own, mirrored))
        own.append(lax.all_to_all(updated, "row", split_axis=0, concat_axis=0, tiled=True))
        for shift in range(n_cols):
            hops = []
            for r in range(n_rows):
                for c in range(n_cols):
                    to = (halves * c + r // n_cols) * n_cols + (r % n_cols ^ shift)
                    hops.append((r * n_cols + c, to))
            mirrored.append(lax.ppermute(turned[shift], AXES, hops))

    spots = jnp.stack([col_at ^ shift for shift in range(n_cols)]).astype(jnp.int32)
    bins = w_pae.shape[1]
    w_both = jnp.concatenate(
        [jnp.pad(w_pae, ((0, 0), (0, bins))), jnp.pad(w_pde, ((0, 0), (bins, 0)))], axis=0
    )
    return pl.pallas_call(
        functools.partial(logits_kernel, n_cols, rounds),
        out_shape=jax.ShapeDtypeStruct((rows_dev, cols_dev, 2 * bins), F32),
        grid_spec=pltpu.PrefetchScalarGridSpec(
            num_scalar_prefetch=1,
            grid=(n_cols,),
            in_specs=[whole(array) for array in own + mirrored + [w_both]],
            out_specs=pl.BlockSpec((slab, cols_dev, 2 * bins), lambda b, at: (at[b], 0, 0)),
            scratch_shapes=[pltpu.VMEM((cols_dev * rows_dev, width), F32)],
        ),
        compiler_params=params,
        name="logits_kernel",
    )(spots, *own, *mirrored, w_both)


def solution(mesh):
    in_specs = (
        P("row", "col", None),
        P(None, ("row", "col")),
        P(("row", "col")),
        P(),
        P(),
        P(),
        P(),
        P(),
        P(),
    )
    out_specs = P("row", "col", None)
    return jax.shard_map(
        per_device, mesh=mesh, in_specs=in_specs, out_specs=out_specs, check_vma=False
    )
```

```python
import functools

import jax
import jax.numpy as jnp
from jax import lax
from jax.experimental import pallas as pl
from jax.experimental.pallas import tpu as pltpu
from jax.sharding import PartitionSpec as P

F32 = jnp.float32
BF16 = jnp.bfloat16
NT = (((1,), (1,)), ((), ()))
VMEM_LIMIT = 56 * 1024 * 1024
AXES = ("row", "col")


def means(parts):
    width = parts[0].shape[-1]
    stacked = jnp.concatenate(parts, axis=1) if len(parts) > 1 else parts[0]
    return jnp.dot(stacked, jnp.full((stacked.shape[1], width), 1.0 / width, BF16), preferred_element_type=F32)


def normalise(values, parts):
    centred = values - means(parts)
    squares = centred * centred
    high = squares.astype(BF16)
    variance = means([high, (squares - high.astype(F32)).astype(BF16)])
    return (centred * lax.rsqrt(variance + 1e-05)).astype(BF16)


def normalise_pair(mine, other):
    width = mine.shape[1]
    row = lax.broadcasted_iota(jnp.int32, (2 * width, 2 * width), 0) < width
    lane = lax.broadcasted_iota(jnp.int32, (2 * width, 2 * width), 1) < width
    both_ways = jnp.where(jnp.logical_or(row, jnp.logical_not(lane)), 1.0 / width, 0.0).astype(BF16)
    each_way = jnp.where(row == lane, 1.0 / width, 0.0).astype(BF16)
    average = jnp.dot(jnp.concatenate([mine.astype(BF16), other], axis=1), both_ways, preferred_element_type=F32)
    centred = jnp.concatenate([mine, mine + other.astype(F32)], axis=1) - average
    squares = centred * centred
    high = squares.astype(BF16)
    rest = (squares - high.astype(F32)).astype(BF16)
    variance = jnp.dot(high, each_way, preferred_element_type=F32) + jnp.dot(rest, each_way, preferred_element_type=F32)
    return (centred * lax.rsqrt(variance + 1e-05)).astype(BF16)


def embed(squares, low, high, w_dist, values):
    hots = []
    for squared in squares:
        inside = (squared > low[...]) & (squared <= high[...])
        hots.append(jnp.where(inside, 1.0, 0.0).astype(BF16))
    hot = jnp.concatenate(hots, axis=0) if len(hots) > 1 else hots[0]
    embedded = jnp.dot(hot, w_dist[...], preferred_element_type=F32)
    return (values + embedded).astype(BF16)


def squared_distance(spread, scalars, token):
    squared = None
    for axis in range(3):
        offset = spread[axis] - scalars[axis, token].astype(F32)
        squared = offset * offset if squared is None else squared + offset * offset
    return squared


def spread_lines(lines, spread):
    length, width = spread.shape[1:]
    for axis in range(3):
        for first in range(0, length, width):
            line = lines[axis : axis + 1, first : first + width].astype(F32)
            spread[axis, first : first + width] = jnp.transpose(jnp.broadcast_to(line, (width, width)))


def bias_kernel(batch, scalars, tokens, low, high, z, w_dist, w_bias, bias, found, spread):
    rows_dev, cols_dev, width = z.shape
    heads = found.shape[0]
    row_at, col_at = lax.axis_index("row"), lax.axis_index("col")
    spread_lines(tokens[:, pl.ds(pl.multiple_of(col_at * cols_dev, cols_dev), cols_dev)], spread)

    def some_rows(step, carry):
        first = step * batch
        values = z[pl.ds(first, batch)].reshape(batch * cols_dev, width).astype(F32)
        squares = [squared_distance(spread, scalars, row_at * rows_dev + first + at) for at in range(batch)]
        pair = embed(squares, low, high, w_dist, values)
        normed = normalise(pair.astype(F32), [pair])
        lines = lax.dot_general(w_bias[...], normed, NT, preferred_element_type=F32)
        for at in range(batch):
            for head in range(heads):
                found[head, pl.ds(first + at, 1), :] = lines[head : head + 1, at * cols_dev : (at + 1) * cols_dev]
        return carry

    lax.fori_loop(0, rows_dev // batch, some_rows, 0)
    swap = row_at % 2 == 1
    for duo in range(heads // 2):
        even, odd = found[2 * duo], found[2 * duo + 1]
        lines = jnp.concatenate([jnp.where(swap, odd, even), jnp.where(swap, even, odd)], axis=0)
        bias[duo] = jnp.transpose(lines)


def project_kernel(
    head_dim, batch, scalars, tokens, low, high, z, w_dist, w_key, w_rest, pair, key, query, value, gate, wide, spread
):
    total, slab, width = z.shape
    row_at, col_at = lax.axis_index("row"), lax.axis_index("col")
    cols_dev = spread.shape[2]
    half = cols_dev // 2

    @pl.when(pl.program_id(0) == 0)
    def _():
        spread_lines(tokens, spread)
        wide[...] = z[...].reshape(total * slab, width).astype(F32)

    first = pl.program_id(0) * batch
    own = col_at * cols_dev + row_at * slab + first
    values = jnp.concatenate([wide[pl.ds(first + at, total, stride=slab), :] for at in range(batch)], axis=0)
    squares = [squared_distance(spread, scalars, own + at) for at in range(batch)]
    rounded = embed(squares, low, high, w_dist, values)
    normed = normalise(rounded.astype(F32), [rounded])
    rest = jnp.dot(normed, w_rest[...], preferred_element_type=F32)
    odd_lane = lax.broadcasted_iota(jnp.int32, (1, width), 1) // head_dim % 2 == 1
    odd_row = lax.broadcasted_iota(jnp.int32, (width, 1), 0) // head_dim % 2 == 1
    for at in range(batch):
        rows = slice(at * total, (at + 1) * total)
        pair[at] = rounded[rows]
        query[at] = (rest[rows, :width] * head_dim ** (-0.5)).astype(BF16)
        gate[at] = rest[rows, 2 * width :].astype(BF16)
        values = rest[rows, width : 2 * width]
        swapped = []
        for start in range(0, total, 2 * half):
            swapped += [values[start + half : start + 2 * half], values[start : start + half]]
        value[at] = jnp.where(odd_lane, jnp.concatenate(swapped, axis=0), values).astype(BF16)
        lines = lax.dot_general(w_key[...], normed[rows], NT, preferred_element_type=F32)
        for start in range(0, total, 2 * half):
            block = lines[:, start : start + 2 * half]
            key[at, :, start : start + 2 * half] = jnp.where(odd_row, pltpu.roll(block, half, 1), block).astype(BF16)


def attention_kernel(heads, n_cols, splits, tokens, key, query, value, gate, pair, w_out, *refs):
    n_rows, count = len(splits), sum(splits)
    bias = [refs[sum(splits[:step]) : sum(splits[: step + 1])] for step in range(n_rows)]
    updated, mirrored, biased, result = refs[count], refs[count + 1 : -2], refs[-2], refs[-1]
    width, total = key.shape[1:]
    cols_dev = bias[0][0].shape[2]
    rows_dev = updated.shape[2]
    halves = n_rows // n_cols
    head_dim = width // heads
    row_at, col_at = lax.axis_index("row"), lax.axis_index("col")
    lane = lax.broadcasted_iota(jnp.int32, (1, width), 1)

    @pl.when(pl.program_id(0) == 0)
    def _():
        from_own = (lane < rows_dev) != (row_at % 2 == 1)
        for step in range(0, n_rows, 2):
            spot = (row_at ^ step) // 2
            start = pl.multiple_of(spot * cols_dev, cols_dev)
            mask = (tokens[3:4, pl.ds(start, cols_dev)].astype(F32) - 1.0) * 30000.0
            for duo in range(heads // 2):
                masks = [mask, jnp.concatenate([mask[:, rows_dev:], mask[:, :rows_dev]], axis=1)]
                for block in range(n_cols):
                    piece, spot_in = divmod(block, n_cols // splits[step])
                    tiles = bias[step][piece][spot_in, duo], bias[step + 1][piece][spot_in, duo]
                    rows = pl.ds(pl.multiple_of((col_at ^ block) * cols_dev, cols_dev), cols_dev)
                    biased[spot, 2 * duo, rows] = jnp.where(from_own, tiles[0], tiles[1]) + masks[0]
                    biased[spot, 2 * duo + 1, rows] = jnp.where(from_own, tiles[1], tiles[0]) + masks[1]

    own_key, own_query = key[0], query[0]
    own_value = jnp.concatenate([value[0], jnp.ones((total, width), BF16)], axis=1)
    blocks = [jnp.zeros((cols_dev, width), F32)] * (total // cols_dev)
    for head in range(heads):
        inside = lane // head_dim == head
        for at in range(len(blocks)):
            rows = slice(at * cols_dev, (at + 1) * cols_dev)
            own = jnp.where(inside, own_query[rows], jnp.zeros((), BF16))
            score = jnp.dot(own, own_key, preferred_element_type=F32)
            score = score + jnp.concatenate([biased[spot, head, rows] for spot in range(biased.shape[0])], axis=1)
            highest = jnp.max(score, axis=1, keepdims=True)
            raised = jnp.exp(score - highest).astype(BF16)
            summed = jnp.dot(raised, own_value, preferred_element_type=F32)
            blocks[at] = jnp.where(inside, summed[:, :width] / summed[:, width:], blocks[at])
    attended = jnp.concatenate(blocks, axis=0)
    gated = (jax.nn.sigmoid(gate[0].astype(F32)) * attended).astype(BF16)
    update = jnp.dot(gated, w_out[...], preferred_element_type=F32)
    result[...] = (pair[0].astype(F32) + update).astype(BF16).reshape(result.shape)
    updated[:, 0] = result[...]
    for shift in range(n_cols):
        block = (row_at % n_cols) ^ shift
        mirrored[shift][:, 0] = result[pl.ds(block * halves, halves)]


def logits_kernel(n_cols, rounds, *refs):
    own = refs[1 : 1 + rounds]
    mirrored = refs[1 + rounds : 1 + rounds + rounds * n_cols]
    w_both, logits, wide = refs[1 + rounds + rounds * n_cols :]
    n_rows, part, rows_dev, width = own[0].shape
    halves = n_rows // n_cols
    cols_dev = halves * rows_dev
    slab = rounds * part
    at_shift = pl.program_id(0)

    @pl.when(at_shift == 0)
    def _():
        size = part * rows_dev
        for row in range(n_rows):
            for step in range(rounds):
                first = (row * rounds + step) * size
                wide[first : first + size, :] = own[step][row].reshape(size, width).astype(F32)

    first = refs[0][at_shift] * slab
    for shift in range(n_cols):

        @pl.when(at_shift == shift)
        def _():
            for step in range(rounds):
                mine, other = [], []
                for at in range(part):
                    mine.append(wide[pl.ds(first + step * part + at, cols_dev, stride=rows_dev), :])
                    other += [mirrored[step * n_cols + shift][half, at] for half in range(halves)]
                mine, other = jnp.concatenate(mine, axis=0), jnp.concatenate(other, axis=0)
                both = normalise_pair(mine, other)
                found = jnp.dot(both, w_both[...], preferred_element_type=F32)
                logits[step * part : (step + 1) * part] = found.reshape(part, cols_dev, found.shape[1])


def swap_over(array, axis, step, count):
    return lax.ppermute(array, axis, [(at, at ^ step) for at in range(count)])


def per_device(z_trunk, coords, token_mask, w_dist, w_attn, w_bias, w_out, w_pae, w_pde):
    rows_dev, cols_dev, width = z_trunk.shape
    n_rows, n_cols = lax.axis_size("row"), lax.axis_size("col")
    total = rows_dev * n_rows
    slab = rows_dev // n_cols
    halves = cols_dev // rows_dev
    heads = w_bias.shape[1]
    head_dim = width // heads
    classes = w_dist.shape[0]
    row_at, col_at = lax.axis_index("row"), lax.axis_index("col")
    params = pltpu.CompilerParams(vmem_limit_bytes=VMEM_LIMIT)
    vmem = pl.BlockSpec(memory_space=pltpu.VMEM)
    smem = pl.BlockSpec(memory_space=pltpu.SMEM)
    once = pl.Buffered(1)
    whole = lambda array: pl.BlockSpec(array.shape, lambda *at: (0,) * array.ndim, pipeline_mode=once)

    edges = (27.0 + 4.0 * jnp.arange(classes - 1, dtype=F32)) ** 2
    low = jnp.concatenate([jnp.full((1,), -1.0, F32), edges, jnp.full((width - classes,), 1e9, F32)])[None]
    high = jnp.concatenate([edges, jnp.full((width - classes + 1,), 1e9, F32)])[None]
    w_dist_full = jnp.pad(w_dist, ((0, width - classes), (0, 0)))
    w_bias_t = jnp.pad(w_bias.T, ((0, 16 - heads), (0, 0)))

    tokens = jnp.concatenate([coords, token_mask[None, :]], axis=0)
    copies = jnp.broadcast_to(tokens[None], (n_rows * n_cols,) + tokens.shape)
    tokens = lax.all_to_all(copies, AXES, split_axis=0, concat_axis=0, tiled=True)
    tokens = tokens.transpose(1, 0, 2).reshape(4, total)
    z_parts = z_trunk.reshape(rows_dev, n_rows, slab, width).swapaxes(0, 1)
    z_parts, w_dist_full, w_bias_t = lax.optimization_barrier((z_parts, w_dist_full, w_bias_t))
    z_cols = lax.all_to_all(z_parts, "row", split_axis=0, concat_axis=0, tiled=True)
    z_cols = z_cols.reshape(total, slab, width)

    bias = pl.pallas_call(
        functools.partial(bias_kernel, 16),
        out_shape=jax.ShapeDtypeStruct((heads // 2, cols_dev, 2 * rows_dev), F32),
        in_specs=[smem] + [vmem] * 6,
        out_specs=vmem,
        scratch_shapes=[pltpu.VMEM((heads, rows_dev, cols_dev), F32), pltpu.VMEM((3, cols_dev, width), F32)],
        compiler_params=params,
        cost_estimate=pl.CostEstimate(flops=rows_dev * cols_dev * width * 300, bytes_accessed=1 << 22, transcendentals=0),
        name="bias_kernel",
    )(tokens, tokens, low, high, z_trunk, w_dist_full, w_bias_t)

    plane = jnp.stack([bias] + [swap_over(bias, "col", step, n_cols) for step in range(1, n_cols)])
    held = {0: [plane]}
    for step in range(2, n_rows, 2):
        if step & (step - 1) == 0:
            held[step] = [swap_over(plane, "row", step, n_rows)]

    w_key = w_attn[:, width : 2 * width].T
    w_rest = jnp.concatenate([w_attn[:, :width], w_attn[:, 2 * width :]], axis=1)
    batch = 4
    by_rows = pl.BlockSpec((batch, total, width), lambda j: (j, 0, 0))
    by_lanes = pl.BlockSpec((batch, width, total), lambda j: (j, 0, 0))
    rows_shape = jax.ShapeDtypeStruct((slab, total, width), BF16)
    lanes_shape = jax.ShapeDtypeStruct((slab, width, total), BF16)
    projected = pl.pallas_call(
        functools.partial(project_kernel, head_dim, batch),
        out_shape=(rows_shape, lanes_shape, rows_shape, rows_shape, rows_shape),
        grid=(slab // batch,),
        in_specs=[smem, whole(tokens), vmem, vmem, whole(z_cols), vmem, vmem, vmem],
        out_specs=(by_rows, by_lanes, by_rows, by_rows, by_rows),
        scratch_shapes=[pltpu.VMEM((total * slab, width), F32), pltpu.VMEM((3, total, width), F32)],
        compiler_params=params,
        cost_estimate=pl.CostEstimate(flops=total * slab * width * 2000, bytes_accessed=1 << 24, transcendentals=0),
        name="project_kernel",
    )(tokens, tokens, low, high, z_cols, w_dist_full, w_key, w_rest)
    held, projected = lax.optimization_barrier((held, projected))
    for step in range(2, n_rows, 2):
        one = step & -step
        if step != one:
            cut = n_cols // 2
            first, second = held[step ^ one], held[one]
            first = first[0] if len(first) == 2 else first[0][:cut]
            second = second[1] if len(second) == 2 else second[0][cut:]
            held[step] = [swap_over(first, "row", one, n_rows), swap_over(second, "row", step ^ one, n_rows)]
    for step in range(0, n_rows, 2):
        held[step + 1] = [swap_over(tile, "row", 1, n_rows) for tile in held[step]]
    splits = tuple(len(held[step]) for step in range(n_rows))
    tiles = [tile for step in range(n_rows) for tile in held[step]]
    pair, key, query, value, gate = projected

    rounds = 2
    part = slab // rounds
    own, mirrored = [], []
    for step in range(rounds):
        rows_spec = pl.BlockSpec((1, total, width), lambda j, step=step: (j + step * part, 0, 0))
        lanes_spec = pl.BlockSpec((1, width, total), lambda j, step=step: (j + step * part, 0, 0))
        out_spec = lambda count: pl.BlockSpec((count, 1, rows_dev, width), lambda j: (0, j, 0, 0))
        out_shape = lambda count: jax.ShapeDtypeStruct((count, part, rows_dev, width), BF16)
        updated, *turned = pl.pallas_call(
            functools.partial(attention_kernel, heads, n_cols, splits),
            out_shape=(out_shape(n_rows),) + (out_shape(halves),) * n_cols,
            grid=(part,),
            in_specs=[whole(tokens), lanes_spec, rows_spec, rows_spec, rows_spec, rows_spec, whole(w_out)]
            + [whole(tile) for tile in tiles],
            out_specs=(out_spec(n_rows),) + (out_spec(halves),) * n_cols,
            scratch_shapes=[
                pltpu.VMEM((total // cols_dev, heads, total, cols_dev), F32),
                pltpu.VMEM((n_rows, rows_dev, width), BF16),
            ],
            compiler_params=params,
            cost_estimate=pl.CostEstimate(
                flops=4 * part * total * total * heads * 256,
                bytes_accessed=1 << 24,
                transcendentals=part * heads * total * total,
            ),
            name="attention_kernel",
        )(tokens, key, query, value, gate, pair, w_out, *tiles)
        if step:
            updated, turned, own, mirrored = lax.optimization_barrier((updated, turned, own, mirrored))
        own.append(lax.all_to_all(updated, "row", split_axis=0, concat_axis=0, tiled=True))
        for shift in range(n_cols):
            hops = []
            for r in range(n_rows):
                for c in range(n_cols):
                    to = (halves * c + r // n_cols) * n_cols + (r % n_cols ^ shift)
                    hops.append((r * n_cols + c, to))
            mirrored.append(lax.ppermute(turned[shift], AXES, hops))

    spots = jnp.stack([col_at ^ shift for shift in range(n_cols)]).astype(jnp.int32)
    bins = w_pae.shape[1]
    w_both = jnp.concatenate(
        [jnp.pad(w_pae, ((0, 0), (0, bins))), jnp.pad(w_pde, ((0, 0), (bins, 0)))], axis=0
    )
    return pl.pallas_call(
        functools.partial(logits_kernel, n_cols, rounds),
        out_shape=jax.ShapeDtypeStruct((rows_dev, cols_dev, 2 * bins), F32),
        grid_spec=pltpu.PrefetchScalarGridSpec(
            num_scalar_prefetch=1,
            grid=(n_cols,),
            in_specs=[whole(array) for array in own + mirrored + [w_both]],
            out_specs=pl.BlockSpec((slab, cols_dev, 2 * bins), lambda b, at: (at[b], 0, 0)),
            scratch_shapes=[pltpu.VMEM((cols_dev * rows_dev, width), F32)],
        ),
        compiler_params=params,
        name="logits_kernel",
    )(spots, *own, *mirrored, w_both)


def solution(mesh):
    in_specs = (
        P("row", "col", None),
        P(None, ("row", "col")),
        P(("row", "col")),
        P(),
        P(),
        P(),
        P(),
        P(),
        P(),
    )
    out_specs = P("row", "col", None)
    return jax.shard_map(
        per_device, mesh=mesh, in_specs=in_specs, out_specs=out_specs, check_vma=False
    )
```

```python
import functools

import jax
import jax.numpy as jnp
from jax import lax
from jax.experimental import pallas as pl
from jax.experimental.pallas import tpu as pltpu
from jax.sharding import PartitionSpec as P

F32 = jnp.float32
BF16 = jnp.bfloat16
NT = (((1,), (1,)), ((), ()))
VMEM_LIMIT = 56 * 1024 * 1024
AXES = ("row", "col")


def normalise(values):
    average = jnp.mean(values, axis=-1, keepdims=True)
    centred = values - average
    variance = jnp.mean(centred * centred, axis=-1, keepdims=True)
    return (centred * lax.rsqrt(variance + 1e-05)).astype(BF16)


def embed(squares, low, high, w_dist, values):
    hots = []
    for squared in squares:
        inside = (squared > low[...]) & (squared <= high[...])
        hots.append(jnp.where(inside, 1.0, 0.0).astype(BF16))
    hot = jnp.concatenate(hots, axis=0) if len(hots) > 1 else hots[0]
    embedded = jnp.dot(hot, w_dist[...], preferred_element_type=F32)
    return (values + embedded).astype(BF16)


def squared_distance(spread, scalars, token):
    squared = None
    for axis in range(3):
        offset = spread[axis] - scalars[axis, token].astype(F32)
        squared = offset * offset if squared is None else squared + offset * offset
    return squared


def spread_lines(lines, spread):
    length, width = spread.shape[1:]
    for axis in range(3):
        for first in range(0, length, width):
            line = lines[axis : axis + 1, first : first + width].astype(F32)
            spread[axis, first : first + width] = jnp.transpose(jnp.broadcast_to(line, (width, width)))


def bias_kernel(batch, scalars, tokens, low, high, z, w_dist, w_bias, bias, found, spread):
    rows_dev, cols_dev, width = z.shape
    heads = found.shape[0]
    row_at, col_at = lax.axis_index("row"), lax.axis_index("col")
    spread_lines(tokens[:, pl.ds(pl.multiple_of(col_at * cols_dev, cols_dev), cols_dev)], spread)

    def some_rows(step, carry):
        first = step * batch
        values = z[pl.ds(first, batch)].reshape(batch * cols_dev, width).astype(F32)
        squares = [squared_distance(spread, scalars, row_at * rows_dev + first + at) for at in range(batch)]
        pair = embed(squares, low, high, w_dist, values)
        normed = normalise(pair.astype(F32))
        lines = lax.dot_general(w_bias[...], normed, NT, preferred_element_type=F32)
        for at in range(batch):
            for head in range(heads):
                found[head, pl.ds(first + at, 1), :] = lines[head : head + 1, at * cols_dev : (at + 1) * cols_dev]
        return carry

    lax.fori_loop(0, rows_dev // batch, some_rows, 0)
    swap = row_at % 2 == 1
    for duo in range(heads // 2):
        even, odd = found[2 * duo], found[2 * duo + 1]
        lines = jnp.concatenate([jnp.where(swap, odd, even), jnp.where(swap, even, odd)], axis=0)
        bias[duo] = jnp.transpose(lines)


def project_kernel(
    head_dim, batch, done, part, scalars, tokens, low, high, z, w_dist, w_key, w_rest, pair, key, query, value, gate, wide, spread
):
    total, slab, width = z.shape
    row_at, col_at = lax.axis_index("row"), lax.axis_index("col")
    cols_dev = spread.shape[2]
    half = cols_dev // 2
    pitch = wide.shape[0] // total
    lowest = done // 8 * 8

    @pl.when(pl.program_id(0) == 0)
    def _():
        spread_lines(tokens, spread)
        lines = 16

        def some_lines(step, carry):
            for at in range(lines):
                spot = pl.multiple_of((step * lines + at) * pitch, 8)
                wide[pl.ds(spot, pitch), :] = z[step * lines + at].astype(F32)[lowest : lowest + pitch]
            return carry

        lax.fori_loop(0, total // lines, some_lines, 0)

    first = pl.program_id(0) * batch
    own = col_at * cols_dev + row_at * slab + done + first
    values = jnp.concatenate([wide[pl.ds(done - lowest + first + at, total, stride=pitch), :] for at in range(batch)], axis=0)
    squares = [squared_distance(spread, scalars, own + at) for at in range(batch)]
    rounded = embed(squares, low, high, w_dist, values)
    normed = normalise(rounded.astype(F32))
    rest = jnp.dot(normed, w_rest[...], preferred_element_type=F32)
    odd_lane = lax.broadcasted_iota(jnp.int32, (1, width), 1) // head_dim % 2 == 1
    odd_row = lax.broadcasted_iota(jnp.int32, (width, 1), 0) // head_dim % 2 == 1
    for at in range(batch):
        rows = slice(at * total, (at + 1) * total)
        pair[at] = rounded[rows]
        query[at] = (rest[rows, :width] * head_dim ** (-0.5)).astype(BF16)
        gate[at] = rest[rows, 2 * width :].astype(BF16)
        values = rest[rows, width : 2 * width]
        swapped = []
        for start in range(0, total, 2 * half):
            swapped += [values[start + half : start + 2 * half], values[start : start + half]]
        value[at] = jnp.where(odd_lane, jnp.concatenate(swapped, axis=0), values).astype(BF16)
        lines = lax.dot_general(w_key[...], normed[rows], NT, preferred_element_type=F32)
        for start in range(0, total, 2 * half):
            block = lines[:, start : start + 2 * half]
            key[at, :, start : start + 2 * half] = jnp.where(odd_row, pltpu.roll(block, half, 1), block).astype(BF16)


def attention_kernel(heads, n_cols, splits, tokens, key, query, value, gate, pair, w_out, *refs):
    n_rows, count = len(splits), sum(splits)
    bias = [refs[sum(splits[:step]) : sum(splits[: step + 1])] for step in range(n_rows)]
    updated, mirrored, biased, result = refs[count], refs[count + 1 : -2], refs[-2], refs[-1]
    width, total = key.shape[1:]
    cols_dev = bias[0][0].shape[2]
    rows_dev = updated.shape[2]
    halves = n_rows // n_cols
    head_dim = width // heads
    row_at, col_at = lax.axis_index("row"), lax.axis_index("col")
    lane = lax.broadcasted_iota(jnp.int32, (1, width), 1)

    @pl.when(pl.program_id(0) == 0)
    def _():
        from_own = (lane < rows_dev) != (row_at % 2 == 1)
        for step in range(0, n_rows, 2):
            spot = (row_at ^ step) // 2
            start = pl.multiple_of(spot * cols_dev, cols_dev)
            mask = (tokens[3:4, pl.ds(start, cols_dev)].astype(F32) - 1.0) * 30000.0
            for duo in range(heads // 2):
                masks = [mask, jnp.concatenate([mask[:, rows_dev:], mask[:, :rows_dev]], axis=1)]
                for block in range(n_cols):
                    piece, spot_in = divmod(block, n_cols // splits[step])
                    tiles = bias[step][piece][spot_in, duo], bias[step + 1][piece][spot_in, duo]
                    rows = pl.ds(pl.multiple_of((col_at ^ block) * cols_dev, cols_dev), cols_dev)
                    biased[spot, 2 * duo, rows] = jnp.where(from_own, tiles[0], tiles[1]) + masks[0]
                    biased[spot, 2 * duo + 1, rows] = jnp.where(from_own, tiles[1], tiles[0]) + masks[1]

    own_key, own_query = key[0], query[0]
    own_value = jnp.concatenate([value[0], jnp.ones((total, width), BF16)], axis=1)
    blocks = [jnp.zeros((cols_dev, width), F32)] * (total // cols_dev)
    for head in range(heads):
        inside = lane // head_dim == head
        for at in range(len(blocks)):
            rows = slice(at * cols_dev, (at + 1) * cols_dev)
            own = jnp.where(inside, own_query[rows], jnp.zeros((), BF16))
            score = jnp.dot(own, own_key, preferred_element_type=F32)
            score = score + jnp.concatenate([biased[spot, head, rows] for spot in range(biased.shape[0])], axis=1)
            highest = jnp.max(score, axis=1, keepdims=True)
            raised = jnp.exp(score - highest).astype(BF16)
            summed = jnp.dot(raised, own_value, preferred_element_type=F32)
            blocks[at] = jnp.where(inside, summed[:, :width] / summed[:, width:], blocks[at])
    attended = jnp.concatenate(blocks, axis=0)
    gated = (jax.nn.sigmoid(gate[0].astype(F32)) * attended).astype(BF16)
    update = jnp.dot(gated, w_out[...], preferred_element_type=F32)
    result[...] = (pair[0].astype(F32) + update).astype(BF16).reshape(result.shape)
    updated[:, 0] = result[...]
    for shift in range(n_cols):
        block = (row_at % n_cols) ^ shift
        mirrored[shift][:, 0] = result[pl.ds(block * halves, halves)]


def logits_kernel(n_cols, parts, *refs):
    rounds = len(parts)
    own = refs[1 : 1 + rounds]
    mirrored = refs[1 + rounds : 1 + rounds + rounds * n_cols]
    w_both, logits, wide = refs[1 + rounds + rounds * n_cols :]
    n_rows, _, rows_dev, width = own[0].shape
    halves = n_rows // n_cols
    cols_dev = halves * rows_dev
    slab = sum(parts)
    pitch = wide.shape[0] // cols_dev
    at_shift = pl.program_id(0)

    @pl.when(at_shift == 0)
    def _():
        for row in range(n_rows):
            for step in range(rounds):
                for at in range(parts[step]):
                    first = (row * slab + sum(parts[:step]) + at) * pitch
                    wide[first : first + rows_dev, :] = own[step][row, at].astype(F32)

    first = refs[0][at_shift] * slab
    for shift in range(n_cols):

        @pl.when(at_shift == shift)
        def _():
            for step in range(rounds):
                done = sum(parts[:step])
                mine, other = [], []
                for at in range(parts[step]):
                    mine.append(wide[pl.ds(first + done + at, cols_dev, stride=pitch), :])
                    other += [mirrored[step * n_cols + shift][half, at] for half in range(halves)]
                mine, other = jnp.concatenate(mine, axis=0), jnp.concatenate(other, axis=0).astype(F32)
                both = jnp.concatenate([normalise(mine), normalise(mine + other)], axis=1)
                found = jnp.dot(both, w_both[...], preferred_element_type=F32)
                logits[done : done + parts[step]] = found.reshape(parts[step], cols_dev, found.shape[1])


def swap_over(array, axis, step, count):
    return lax.ppermute(array, axis, [(at, at ^ step) for at in range(count)])


def per_device(z_trunk, coords, token_mask, w_dist, w_attn, w_bias, w_out, w_pae, w_pde):
    rows_dev, cols_dev, width = z_trunk.shape
    n_rows, n_cols = lax.axis_size("row"), lax.axis_size("col")
    total = rows_dev * n_rows
    slab = rows_dev // n_cols
    halves = cols_dev // rows_dev
    heads = w_bias.shape[1]
    head_dim = width // heads
    classes = w_dist.shape[0]
    row_at, col_at = lax.axis_index("row"), lax.axis_index("col")
    params = pltpu.CompilerParams(vmem_limit_bytes=VMEM_LIMIT)
    vmem = pl.BlockSpec(memory_space=pltpu.VMEM)
    smem = pl.BlockSpec(memory_space=pltpu.SMEM)
    once = pl.Buffered(1)
    whole = lambda array: pl.BlockSpec(array.shape, lambda *at: (0,) * array.ndim, pipeline_mode=once)

    edges = (27.0 + 4.0 * jnp.arange(classes - 1, dtype=F32)) ** 2
    low = jnp.concatenate([jnp.full((1,), -1.0, F32), edges, jnp.full((width - classes,), 1e9, F32)])[None]
    high = jnp.concatenate([edges, jnp.full((width - classes + 1,), 1e9, F32)])[None]
    w_dist_full = jnp.pad(w_dist, ((0, width - classes), (0, 0)))
    w_bias_t = jnp.pad(w_bias.T, ((0, 16 - heads), (0, 0)))

    tokens = jnp.concatenate([coords, token_mask[None, :]], axis=0)
    copies = jnp.broadcast_to(tokens[None], (n_rows * n_cols,) + tokens.shape)
    tokens = lax.all_to_all(copies, AXES, split_axis=0, concat_axis=0, tiled=True)
    tokens = tokens.transpose(1, 0, 2).reshape(4, total)
    z_parts = z_trunk.reshape(rows_dev, n_rows, slab, width).swapaxes(0, 1)
    z_parts, w_dist_full, w_bias_t = lax.optimization_barrier((z_parts, w_dist_full, w_bias_t))
    z_cols = lax.all_to_all(z_parts, "row", split_axis=0, concat_axis=0, tiled=True)
    z_cols = z_cols.reshape(total, slab, width)

    bias = pl.pallas_call(
        functools.partial(bias_kernel, 32),
        out_shape=jax.ShapeDtypeStruct((heads // 2, cols_dev, 2 * rows_dev), F32),
        in_specs=[smem] + [vmem] * 6,
        out_specs=vmem,
        scratch_shapes=[pltpu.VMEM((heads, rows_dev, cols_dev), F32), pltpu.VMEM((3, cols_dev, width), F32)],
        compiler_params=params,
        cost_estimate=pl.CostEstimate(flops=rows_dev * cols_dev * width * 300, bytes_accessed=1 << 22, transcendentals=0),
        name="bias_kernel",
    )(tokens, tokens, low, high, z_trunk, w_dist_full, w_bias_t)

    plane = jnp.stack([bias] + [swap_over(bias, "col", step, n_cols) for step in range(1, n_cols)])
    held = {0: [plane]}
    for step in range(2, n_rows, 2):
        if step & (step - 1) == 0:
            held[step] = [swap_over(plane, "row", step, n_rows)]

    w_key = w_attn[:, width : 2 * width].T
    w_rest = jnp.concatenate([w_attn[:, :width], w_attn[:, 2 * width :]], axis=1)
    rounds = 2
    parts = tuple((slab + rounds - 1 - step) // rounds for step in range(rounds))

    def project(step):
        done, part = sum(parts[:step]), parts[step]
        batch = min(4, part)
        spread_rows = -(-(done + part) // 8) * 8 - done // 8 * 8
        by_rows = pl.BlockSpec((batch, total, width), lambda j: (j, 0, 0))
        by_lanes = pl.BlockSpec((batch, width, total), lambda j: (j, 0, 0))
        rows_shape = jax.ShapeDtypeStruct((part, total, width), BF16)
        lanes_shape = jax.ShapeDtypeStruct((part, width, total), BF16)
        return pl.pallas_call(
            functools.partial(project_kernel, head_dim, batch, done, part),
            out_shape=(rows_shape, lanes_shape, rows_shape, rows_shape, rows_shape),
            grid=(part // batch,),
            in_specs=[smem, whole(tokens), vmem, vmem, whole(z_cols), vmem, vmem, vmem],
            out_specs=(by_rows, by_lanes, by_rows, by_rows, by_rows),
            scratch_shapes=[pltpu.VMEM((total * spread_rows, width), F32), pltpu.VMEM((3, total, width), F32)],
            compiler_params=params,
            cost_estimate=pl.CostEstimate(
                flops=total * part * width * 2000, bytes_accessed=1 << 23, transcendentals=0
            ),
            name="project_kernel",
        )(tokens, tokens, low, high, z_cols, w_dist_full, w_key, w_rest)

    projected = [project(0)]
    held, projected = lax.optimization_barrier((held, projected))
    for step in range(2, n_rows, 2):
        one = step & -step
        if step != one:
            cut = n_cols // 2
            first, second = held[step ^ one], held[one]
            first = first[0] if len(first) == 2 else first[0][:cut]
            second = second[1] if len(second) == 2 else second[0][cut:]
            held[step] = [swap_over(first, "row", one, n_rows), swap_over(second, "row", step ^ one, n_rows)]
    projected.append(project(1))
    passed_on = {step: held[step] for step in range(2, n_rows, 2) if step & (step - 1)}
    passed_on, projected = lax.optimization_barrier((passed_on, projected))
    held |= passed_on
    for step in range(0, n_rows, 2):
        held[step + 1] = [swap_over(tile, "row", 1, n_rows) for tile in held[step]]
    splits = tuple(len(held[step]) for step in range(n_rows))
    tiles = [tile for step in range(n_rows) for tile in held[step]]

    own, mirrored = [], []
    for step, part in enumerate(parts):
        pair, key, query, value, gate = projected[step]
        rows_spec = pl.BlockSpec((1, total, width), lambda j: (j, 0, 0))
        lanes_spec = pl.BlockSpec((1, width, total), lambda j: (j, 0, 0))
        out_spec = lambda count: pl.BlockSpec((count, 1, rows_dev, width), lambda j: (0, j, 0, 0))
        out_shape = lambda count: jax.ShapeDtypeStruct((count, part, rows_dev, width), BF16)
        updated, *turned = pl.pallas_call(
            functools.partial(attention_kernel, heads, n_cols, splits),
            out_shape=(out_shape(n_rows),) + (out_shape(halves),) * n_cols,
            grid=(part,),
            in_specs=[whole(tokens), lanes_spec, rows_spec, rows_spec, rows_spec, rows_spec, whole(w_out)]
            + [whole(tile) for tile in tiles],
            out_specs=(out_spec(n_rows),) + (out_spec(halves),) * n_cols,
            scratch_shapes=[
                pltpu.VMEM((total // cols_dev, heads, total, cols_dev), F32),
                pltpu.VMEM((n_rows, rows_dev, width), BF16),
            ],
            compiler_params=params,
            cost_estimate=pl.CostEstimate(
                flops=4 * part * total * total * heads * 256,
                bytes_accessed=1 << 24,
                transcendentals=part * heads * total * total,
            ),
            name="attention_kernel",
        )(tokens, key, query, value, gate, pair, w_out, *tiles)
        if step:
            updated, turned, own, mirrored = lax.optimization_barrier((updated, turned, own, mirrored))
        own.append(lax.all_to_all(updated, "row", split_axis=0, concat_axis=0, tiled=True))
        for shift in range(n_cols):
            hops = []
            for r in range(n_rows):
                for c in range(n_cols):
                    to = (halves * c + r // n_cols) * n_cols + (r % n_cols ^ shift)
                    hops.append((r * n_cols + c, to))
            mirrored.append(lax.ppermute(turned[shift], AXES, hops))

    spots = jnp.stack([col_at ^ shift for shift in range(n_cols)]).astype(jnp.int32)
    bins = w_pae.shape[1]
    w_both = jnp.concatenate(
        [jnp.pad(w_pae, ((0, 0), (0, bins))), jnp.pad(w_pde, ((0, 0), (bins, 0)))], axis=0
    )
    return pl.pallas_call(
        functools.partial(logits_kernel, n_cols, parts),
        out_shape=jax.ShapeDtypeStruct((rows_dev, cols_dev, 2 * bins), F32),
        grid_spec=pltpu.PrefetchScalarGridSpec(
            num_scalar_prefetch=1,
            grid=(n_cols,),
            in_specs=[whole(array) for array in own + mirrored + [w_both]],
            out_specs=pl.BlockSpec((slab, cols_dev, 2 * bins), lambda b, at: (at[b], 0, 0)),
            scratch_shapes=[pltpu.VMEM((cols_dev * (rows_dev + 8), width), F32)],
        ),
        compiler_params=params,
        name="logits_kernel",
    )(spots, *own, *mirrored, w_both)


def solution(mesh):
    in_specs = (
        P("row", "col", None),
        P(None, ("row", "col")),
        P(("row", "col")),
        P(),
        P(),
        P(),
        P(),
        P(),
        P(),
    )
    out_specs = P("row", "col", None)
    return jax.shard_map(
        per_device, mesh=mesh, in_specs=in_specs, out_specs=out_specs, check_vma=False
    )
```

```python
import functools

import jax
import jax.numpy as jnp
from jax import lax
from jax.experimental import pallas as pl
from jax.experimental.pallas import tpu as pltpu
from jax.sharding import PartitionSpec as P

F32 = jnp.float32
BF16 = jnp.bfloat16
NT = (((1,), (1,)), ((), ()))
VMEM_LIMIT = 56 * 1024 * 1024
AXES = ("row", "col")


def normalise(values, parts):
    width = values.shape[1]
    stacked = jnp.concatenate(parts, axis=1) if len(parts) > 1 else parts[0]
    weight = jnp.full((stacked.shape[1], width), 1.0 / width, BF16)
    centred = values - jnp.dot(stacked, weight, preferred_element_type=F32)
    variance = jnp.mean(centred * centred, axis=-1, keepdims=True)
    return (centred * lax.rsqrt(variance + 1e-05)).astype(BF16)


def embed(squares, low, high, w_dist, values):
    hots = []
    for squared in squares:
        inside = (squared > low[...]) & (squared <= high[...])
        hots.append(jnp.where(inside, 1.0, 0.0).astype(BF16))
    hot = jnp.concatenate(hots, axis=0) if len(hots) > 1 else hots[0]
    embedded = jnp.dot(hot, w_dist[...], preferred_element_type=F32)
    return (values + embedded).astype(BF16)


def squared_distance(spread, scalars, token):
    squared = None
    for axis in range(3):
        offset = spread[axis] - scalars[axis, token].astype(F32)
        squared = offset * offset if squared is None else squared + offset * offset
    return squared


def spread_lines(lines, spread):
    length, width = spread.shape[1:]
    for axis in range(3):
        for first in range(0, length, width):
            line = lines[axis : axis + 1, first : first + width].astype(F32)
            spread[axis, first : first + width] = jnp.transpose(jnp.broadcast_to(line, (width, width)))


def bias_kernel(batch, scalars, tokens, low, high, z, w_dist, w_bias, bias, found, spread):
    rows_dev, cols_dev, width = z.shape
    heads = found.shape[0]
    row_at, col_at = lax.axis_index("row"), lax.axis_index("col")
    spread_lines(tokens[:, pl.ds(pl.multiple_of(col_at * cols_dev, cols_dev), cols_dev)], spread)

    def some_rows(step, carry):
        first = step * batch
        values = z[pl.ds(first, batch)].reshape(batch * cols_dev, width).astype(F32)
        squares = [squared_distance(spread, scalars, row_at * rows_dev + first + at) for at in range(batch)]
        pair = embed(squares, low, high, w_dist, values)
        normed = normalise(pair.astype(F32), [pair])
        lines = lax.dot_general(w_bias[...], normed, NT, preferred_element_type=F32)
        for at in range(batch):
            for head in range(heads):
                found[head, pl.ds(first + at, 1), :] = lines[head : head + 1, at * cols_dev : (at + 1) * cols_dev]
        return carry

    lax.fori_loop(0, rows_dev // batch, some_rows, 0)
    swap = row_at % 2 == 1
    for duo in range(heads // 2):
        even, odd = found[2 * duo], found[2 * duo + 1]
        lines = jnp.concatenate([jnp.where(swap, odd, even), jnp.where(swap, even, odd)], axis=0)
        bias[duo] = jnp.transpose(lines)


def project_kernel(
    head_dim, batch, done, part, scalars, tokens, low, high, z, w_dist, w_key, w_rest, pair, key, query, value, gate, wide, spread
):
    total, slab, width = z.shape
    row_at, col_at = lax.axis_index("row"), lax.axis_index("col")
    cols_dev = spread.shape[2]
    half = cols_dev // 2
    pitch = wide.shape[0] // total
    lowest = done // 8 * 8

    @pl.when(pl.program_id(0) == 0)
    def _():
        spread_lines(tokens, spread)
        lines = 16

        def some_lines(step, carry):
            for at in range(lines):
                spot = pl.multiple_of((step * lines + at) * pitch, 8)
                wide[pl.ds(spot, pitch), :] = z[step * lines + at].astype(F32)[lowest : lowest + pitch]
            return carry

        lax.fori_loop(0, total // lines, some_lines, 0)

    first = pl.program_id(0) * batch
    own = col_at * cols_dev + row_at * slab + done + first
    values = jnp.concatenate([wide[pl.ds(done - lowest + first + at, total, stride=pitch), :] for at in range(batch)], axis=0)
    squares = [squared_distance(spread, scalars, own + at) for at in range(batch)]
    rounded = embed(squares, low, high, w_dist, values)
    normed = normalise(rounded.astype(F32), [rounded])
    rest = jnp.dot(normed, w_rest[...], preferred_element_type=F32)
    odd_lane = lax.broadcasted_iota(jnp.int32, (1, width), 1) // head_dim % 2 == 1
    odd_row = lax.broadcasted_iota(jnp.int32, (width, 1), 0) // head_dim % 2 == 1
    for at in range(batch):
        rows = slice(at * total, (at + 1) * total)
        pair[at] = rounded[rows]
        query[at] = (rest[rows, :width] * head_dim ** (-0.5)).astype(BF16)
        gate[at] = rest[rows, 2 * width :].astype(BF16)
        values = rest[rows, width : 2 * width]
        swapped = []
        for start in range(0, total, 2 * half):
            swapped += [values[start + half : start + 2 * half], values[start : start + half]]
        value[at] = jnp.where(odd_lane, jnp.concatenate(swapped, axis=0), values).astype(BF16)
        lines = lax.dot_general(w_key[...], normed[rows], NT, preferred_element_type=F32)
        for start in range(0, total, 2 * half):
            block = lines[:, start : start + 2 * half]
            key[at, :, start : start + 2 * half] = jnp.where(odd_row, pltpu.roll(block, half, 1), block).astype(BF16)


def attention_kernel(heads, n_cols, splits, tokens, key, query, value, gate, pair, w_out, *refs):
    n_rows, count = len(splits), sum(splits)
    bias = [refs[sum(splits[:step]) : sum(splits[: step + 1])] for step in range(n_rows)]
    updated, mirrored, biased, result = refs[count], refs[count + 1 : -2], refs[-2], refs[-1]
    width, total = key.shape[1:]
    cols_dev = bias[0][0].shape[2]
    rows_dev = updated.shape[2]
    halves = n_rows // n_cols
    head_dim = width // heads
    row_at, col_at = lax.axis_index("row"), lax.axis_index("col")
    lane = lax.broadcasted_iota(jnp.int32, (1, width), 1)

    @pl.when(pl.program_id(0) == 0)
    def _():
        from_own = (lane < rows_dev) != (row_at % 2 == 1)
        for step in range(0, n_rows, 2):
            spot = (row_at ^ step) // 2
            start = pl.multiple_of(spot * cols_dev, cols_dev)
            mask = (tokens[3:4, pl.ds(start, cols_dev)].astype(F32) - 1.0) * 30000.0
            for duo in range(heads // 2):
                masks = [mask, jnp.concatenate([mask[:, rows_dev:], mask[:, :rows_dev]], axis=1)]
                for block in range(n_cols):
                    piece, spot_in = divmod(block, n_cols // splits[step])
                    tiles = bias[step][piece][spot_in, duo], bias[step + 1][piece][spot_in, duo]
                    rows = pl.ds(pl.multiple_of((col_at ^ block) * cols_dev, cols_dev), cols_dev)
                    biased[spot, 2 * duo, rows] = jnp.where(from_own, tiles[0], tiles[1]) + masks[0]
                    biased[spot, 2 * duo + 1, rows] = jnp.where(from_own, tiles[1], tiles[0]) + masks[1]

    own_key, own_query = key[0], query[0]
    own_value = jnp.concatenate([value[0], jnp.ones((total, width), BF16)], axis=1)
    blocks = [jnp.zeros((cols_dev, width), F32)] * (total // cols_dev)
    wholes = list(blocks)
    for head in range(heads):
        inside = lane // head_dim == head
        for at in range(len(blocks)):
            rows = slice(at * cols_dev, (at + 1) * cols_dev)
            own = jnp.where(inside, own_query[rows], jnp.zeros((), BF16))
            score = jnp.dot(own, own_key, preferred_element_type=F32)
            score = score + jnp.concatenate([biased[spot, head, rows] for spot in range(biased.shape[0])], axis=1)
            highest = jnp.max(score, axis=1, keepdims=True)
            raised = jnp.exp(score - highest).astype(BF16)
            summed = jnp.dot(raised, own_value, preferred_element_type=F32)
            blocks[at] = jnp.where(inside, summed[:, :width], blocks[at])
            wholes[at] = jnp.where(inside, summed[:, width:], wholes[at])
    attended = jnp.concatenate(blocks, axis=0) / jnp.concatenate(wholes, axis=0)
    gated = (jax.nn.sigmoid(gate[0].astype(F32)) * attended).astype(BF16)
    update = jnp.dot(gated, w_out[...], preferred_element_type=F32)
    result[...] = (pair[0].astype(F32) + update).astype(BF16).reshape(result.shape)
    updated[:, 0] = result[...]
    for shift in range(n_cols):
        block = (row_at % n_cols) ^ shift
        mirrored[shift][:, 0] = result[pl.ds(block * halves, halves)]


def logits_kernel(n_cols, parts, *refs):
    rounds = len(parts)
    own = refs[1 : 1 + rounds]
    mirrored = refs[1 + rounds : 1 + rounds + rounds * n_cols]
    w_both, logits, wide = refs[1 + rounds + rounds * n_cols :]
    n_rows, _, rows_dev, width = own[0].shape
    halves = n_rows // n_cols
    cols_dev = halves * rows_dev
    slab = sum(parts)
    pitch = wide.shape[0] // cols_dev
    at_shift = pl.program_id(0)

    @pl.when(at_shift == 0)
    def _():
        for row in range(n_rows):
            for step in range(rounds):
                for at in range(parts[step]):
                    first = (row * slab + sum(parts[:step]) + at) * pitch
                    wide[first : first + rows_dev, :] = own[step][row, at].astype(F32)

    first = refs[0][at_shift] * slab
    for shift in range(n_cols):

        @pl.when(at_shift == shift)
        def _():
            for step in range(rounds):
                done = sum(parts[:step])
                mine, other = [], []
                for at in range(parts[step]):
                    mine.append(wide[pl.ds(first + done + at, cols_dev, stride=pitch), :])
                    other += [mirrored[step * n_cols + shift][half, at] for half in range(halves)]
                mine, other = jnp.concatenate(mine, axis=0), jnp.concatenate(other, axis=0)
                short = mine.astype(BF16)
                summed = mine + other.astype(F32)
                both = jnp.concatenate([normalise(mine, [short]), normalise(summed, [short, other])], axis=1)
                found = jnp.dot(both, w_both[...], preferred_element_type=F32)
                logits[done : done + parts[step]] = found.reshape(parts[step], cols_dev, found.shape[1])


def swap_over(array, axis, step, count):
    return lax.ppermute(array, axis, [(at, at ^ step) for at in range(count)])


def per_device(z_trunk, coords, token_mask, w_dist, w_attn, w_bias, w_out, w_pae, w_pde):
    rows_dev, cols_dev, width = z_trunk.shape
    n_rows, n_cols = lax.axis_size("row"), lax.axis_size("col")
    total = rows_dev * n_rows
    slab = rows_dev // n_cols
    halves = cols_dev // rows_dev
    heads = w_bias.shape[1]
    head_dim = width // heads
    classes = w_dist.shape[0]
    row_at, col_at = lax.axis_index("row"), lax.axis_index("col")
    params = pltpu.CompilerParams(vmem_limit_bytes=VMEM_LIMIT)
    vmem = pl.BlockSpec(memory_space=pltpu.VMEM)
    smem = pl.BlockSpec(memory_space=pltpu.SMEM)
    once = pl.Buffered(1)
    whole = lambda array: pl.BlockSpec(array.shape, lambda *at: (0,) * array.ndim, pipeline_mode=once)

    edges = (27.0 + 4.0 * jnp.arange(classes - 1, dtype=F32)) ** 2
    low = jnp.concatenate([jnp.full((1,), -1.0, F32), edges, jnp.full((width - classes,), 1e9, F32)])[None]
    high = jnp.concatenate([edges, jnp.full((width - classes + 1,), 1e9, F32)])[None]
    w_dist_full = jnp.pad(w_dist, ((0, width - classes), (0, 0)))
    w_bias_t = jnp.pad(w_bias.T, ((0, 16 - heads), (0, 0)))

    tokens = jnp.concatenate([coords, token_mask[None, :]], axis=0)
    copies = jnp.broadcast_to(tokens[None], (n_rows * n_cols,) + tokens.shape)
    tokens = lax.all_to_all(copies, AXES, split_axis=0, concat_axis=0, tiled=True)
    tokens = tokens.transpose(1, 0, 2).reshape(4, total)
    z_parts = z_trunk.reshape(rows_dev, n_rows, slab, width).swapaxes(0, 1)
    early = (z_parts, w_dist_full, w_bias_t, low, high)
    z_parts, w_dist_full, w_bias_t, low, high = lax.optimization_barrier(early)
    z_cols = lax.all_to_all(z_parts, "row", split_axis=0, concat_axis=0, tiled=True)
    z_cols = z_cols.reshape(total, slab, width)

    bias = pl.pallas_call(
        functools.partial(bias_kernel, 32),
        out_shape=jax.ShapeDtypeStruct((heads // 2, cols_dev, 2 * rows_dev), F32),
        in_specs=[smem] + [vmem] * 6,
        out_specs=vmem,
        scratch_shapes=[pltpu.VMEM((heads, rows_dev, cols_dev), F32), pltpu.VMEM((3, cols_dev, width), F32)],
        compiler_params=params,
        cost_estimate=pl.CostEstimate(flops=rows_dev * cols_dev * width * 300, bytes_accessed=1 << 22, transcendentals=0),
        name="bias_kernel",
    )(tokens, tokens, low, high, z_trunk, w_dist_full, w_bias_t)

    plane = jnp.stack([bias] + [swap_over(bias, "col", step, n_cols) for step in range(1, n_cols)])
    held = {0: [plane]}
    for step in range(2, n_rows, 2):
        if step & (step - 1) == 0:
            held[step] = [swap_over(plane, "row", step, n_rows)]

    w_key = w_attn[:, width : 2 * width].T
    w_rest = jnp.concatenate([w_attn[:, :width], w_attn[:, 2 * width :]], axis=1)
    rounds = 2
    parts = tuple((slab + rounds - 1 - step) // rounds for step in range(rounds))

    def project(step):
        done, part = sum(parts[:step]), parts[step]
        batch = min(4, part)
        spread_rows = -(-(done + part) // 8) * 8 - done // 8 * 8
        by_rows = pl.BlockSpec((batch, total, width), lambda j: (j, 0, 0))
        by_lanes = pl.BlockSpec((batch, width, total), lambda j: (j, 0, 0))
        rows_shape = jax.ShapeDtypeStruct((part, total, width), BF16)
        lanes_shape = jax.ShapeDtypeStruct((part, width, total), BF16)
        return pl.pallas_call(
            functools.partial(project_kernel, head_dim, batch, done, part),
            out_shape=(rows_shape, lanes_shape, rows_shape, rows_shape, rows_shape),
            grid=(part // batch,),
            in_specs=[smem, whole(tokens), vmem, vmem, whole(z_cols), vmem, vmem, vmem],
            out_specs=(by_rows, by_lanes, by_rows, by_rows, by_rows),
            scratch_shapes=[pltpu.VMEM(((total + 1) * spread_rows, width), F32), pltpu.VMEM((3, total, width), F32)],
            compiler_params=params,
            cost_estimate=pl.CostEstimate(
                flops=total * part * width * 2000, bytes_accessed=1 << 23, transcendentals=0
            ),
            name="project_kernel",
        )(tokens, tokens, low, high, z_cols, w_dist_full, w_key, w_rest)

    projected = [project(0)]
    held, projected = lax.optimization_barrier((held, projected))
    for step in range(2, n_rows, 2):
        one = step & -step
        if step != one:
            cut = n_cols // 2
            first, second = held[step ^ one], held[one]
            first = first[0] if len(first) == 2 else first[0][:cut]
            second = second[1] if len(second) == 2 else second[0][cut:]
            held[step] = [swap_over(first, "row", one, n_rows), swap_over(second, "row", step ^ one, n_rows)]
    projected.append(project(1))
    passed_on = {step: held[step] for step in range(2, n_rows, 2) if step & (step - 1)}
    passed_on, projected = lax.optimization_barrier((passed_on, projected))
    held |= passed_on
    for step in range(0, n_rows, 2):
        held[step + 1] = [swap_over(tile, "row", 1, n_rows) for tile in held[step]]
    splits = tuple(len(held[step]) for step in range(n_rows))
    tiles = [tile for step in range(n_rows) for tile in held[step]]

    own, mirrored = [], []
    for step, part in enumerate(parts):
        pair, key, query, value, gate = projected[step]
        rows_spec = pl.BlockSpec((1, total, width), lambda j: (j, 0, 0))
        lanes_spec = pl.BlockSpec((1, width, total), lambda j: (j, 0, 0))
        out_spec = lambda count: pl.BlockSpec((count, 1, rows_dev, width), lambda j: (0, j, 0, 0))
        out_shape = lambda count: jax.ShapeDtypeStruct((count, part, rows_dev, width), BF16)
        updated, *turned = pl.pallas_call(
            functools.partial(attention_kernel, heads, n_cols, splits),
            out_shape=(out_shape(n_rows),) + (out_shape(halves),) * n_cols,
            grid=(part,),
            in_specs=[whole(tokens), lanes_spec, rows_spec, rows_spec, rows_spec, rows_spec, whole(w_out)]
            + [whole(tile) for tile in tiles],
            out_specs=(out_spec(n_rows),) + (out_spec(halves),) * n_cols,
            scratch_shapes=[
                pltpu.VMEM((total // cols_dev, heads, total, cols_dev), F32),
                pltpu.VMEM((n_rows, rows_dev, width), BF16),
            ],
            compiler_params=params,
            cost_estimate=pl.CostEstimate(
                flops=4 * part * total * total * heads * 256,
                bytes_accessed=1 << 24,
                transcendentals=part * heads * total * total,
            ),
            name="attention_kernel",
        )(tokens, key, query, value, gate, pair, w_out, *tiles)
        if step:
            updated, turned, own, mirrored = lax.optimization_barrier((updated, turned, own, mirrored))
        own.append(lax.all_to_all(updated, "row", split_axis=0, concat_axis=0, tiled=True))
        for shift in range(n_cols):
            hops = []
            for r in range(n_rows):
                for c in range(n_cols):
                    to = (halves * c + r // n_cols) * n_cols + (r % n_cols ^ shift)
                    hops.append((r * n_cols + c, to))
            mirrored.append(lax.ppermute(turned[shift], AXES, hops))

    spots = jnp.stack([col_at ^ shift for shift in range(n_cols)]).astype(jnp.int32)
    bins = w_pae.shape[1]
    w_both = jnp.concatenate(
        [jnp.pad(w_pae, ((0, 0), (0, bins))), jnp.pad(w_pde, ((0, 0), (bins, 0)))], axis=0
    )
    return pl.pallas_call(
        functools.partial(logits_kernel, n_cols, parts),
        out_shape=jax.ShapeDtypeStruct((rows_dev, cols_dev, 2 * bins), F32),
        grid_spec=pltpu.PrefetchScalarGridSpec(
            num_scalar_prefetch=1,
            grid=(n_cols,),
            in_specs=[whole(array) for array in own + mirrored + [w_both]],
            out_specs=pl.BlockSpec((slab, cols_dev, 2 * bins), lambda b, at: (at[b], 0, 0)),
            scratch_shapes=[pltpu.VMEM(((cols_dev + 1) * (rows_dev + 8), width), F32)],
        ),
        compiler_params=params,
        name="logits_kernel",
    )(spots, *own, *mirrored, w_both)


def solution(mesh):
    in_specs = (
        P("row", "col", None),
        P(None, ("row", "col")),
        P(("row", "col")),
        P(),
        P(),
        P(),
        P(),
        P(),
        P(),
    )
    out_specs = P("row", "col", None)
    return jax.shard_map(
        per_device, mesh=mesh, in_specs=in_specs, out_specs=out_specs, check_vma=False
    )
```

```python
import functools

import jax
import jax.numpy as jnp
from jax import lax
from jax.experimental import pallas as pl
from jax.experimental.pallas import tpu as pltpu
from jax.sharding import PartitionSpec as P

F32 = jnp.float32
BF16 = jnp.bfloat16
NT = (((1,), (1,)), ((), ()))
VMEM_LIMIT = 56 * 1024 * 1024
AXES = ("row", "col")


def normalise(values, parts):
    width = values.shape[1]
    stacked = jnp.concatenate(parts, axis=1) if len(parts) > 1 else parts[0]
    weight = jnp.full((stacked.shape[1], width), 1.0 / width, BF16)
    centred = values - jnp.dot(stacked, weight, preferred_element_type=F32)
    variance = jnp.mean(centred * centred, axis=-1, keepdims=True)
    return (centred * lax.rsqrt(variance + 1e-05)).astype(BF16)


def embed(squares, low, high, w_dist, values):
    hots = []
    for squared in squares:
        inside = (squared > low[...]) & (squared <= high[...])
        hots.append(jnp.where(inside, 1.0, 0.0).astype(BF16))
    hot = jnp.concatenate(hots, axis=0) if len(hots) > 1 else hots[0]
    embedded = jnp.dot(hot, w_dist[...], preferred_element_type=F32)
    return (values + embedded).astype(BF16)


def squared_distance(spread, scalars, token):
    squared = None
    for axis in range(3):
        offset = spread[axis] - scalars[axis, token].astype(F32)
        squared = offset * offset if squared is None else squared + offset * offset
    return squared


def spread_lines(lines, spread):
    length, width = spread.shape[1:]
    for axis in range(3):
        for first in range(0, length, width):
            line = lines[axis : axis + 1, first : first + width].astype(F32)
            spread[axis, first : first + width] = jnp.transpose(jnp.broadcast_to(line, (width, width)))


def bias_kernel(batch, scalars, tokens, low, high, z, w_dist, w_bias, bias, found, spread):
    rows_dev, cols_dev, width = z.shape
    heads = found.shape[0]
    row_at, col_at = lax.axis_index("row"), lax.axis_index("col")
    spread_lines(tokens[:, pl.ds(pl.multiple_of(col_at * cols_dev, cols_dev), cols_dev)], spread)

    def some_rows(step, carry):
        first = step * batch
        values = z[pl.ds(first, batch)].reshape(batch * cols_dev, width).astype(F32)
        squares = [squared_distance(spread, scalars, row_at * rows_dev + first + at) for at in range(batch)]
        pair = embed(squares, low, high, w_dist, values)
        normed = normalise(pair.astype(F32), [pair])
        lines = lax.dot_general(w_bias[...], normed, NT, preferred_element_type=F32)
        for at in range(batch):
            for head in range(heads):
                found[head, pl.ds(first + at, 1), :] = lines[head : head + 1, at * cols_dev : (at + 1) * cols_dev]
        return carry

    lax.fori_loop(0, rows_dev // batch, some_rows, 0)
    swap = row_at % 2 == 1
    for duo in range(heads // 2):
        even, odd = found[2 * duo], found[2 * duo + 1]
        lines = jnp.concatenate([jnp.where(swap, odd, even), jnp.where(swap, even, odd)], axis=0)
        bias[duo] = jnp.transpose(lines)


def project_kernel(
    head_dim, batch, done, part, scalars, tokens, low, high, z, w_dist, w_key, w_rest, pair, key, query, value, gate, wide, spread
):
    total, slab, width = z.shape
    row_at, col_at = lax.axis_index("row"), lax.axis_index("col")
    cols_dev = spread.shape[2]
    half = cols_dev // 2
    pitch = wide.shape[0] // total
    lowest = done // 8 * 8

    @pl.when(pl.program_id(0) == 0)
    def _():
        spread_lines(tokens, spread)
        lines = 16

        def some_lines(step, carry):
            for at in range(lines):
                spot = pl.multiple_of((step * lines + at) * pitch, 8)
                wide[pl.ds(spot, pitch), :] = z[step * lines + at].astype(F32)[lowest : lowest + pitch]
            return carry

        lax.fori_loop(0, total // lines, some_lines, 0)

    first = pl.program_id(0) * batch
    own = col_at * cols_dev + row_at * slab + done + first
    values = jnp.concatenate([wide[pl.ds(done - lowest + first + at, total, stride=pitch), :] for at in range(batch)], axis=0)
    squares = [squared_distance(spread, scalars, own + at) for at in range(batch)]
    rounded = embed(squares, low, high, w_dist, values)
    normed = normalise(rounded.astype(F32), [rounded])
    rest = jnp.dot(normed, w_rest[...], preferred_element_type=F32)
    odd_lane = lax.broadcasted_iota(jnp.int32, (1, width), 1) // head_dim % 2 == 1
    odd_row = lax.broadcasted_iota(jnp.int32, (width, 1), 0) // head_dim % 2 == 1
    for at in range(batch):
        rows = slice(at * total, (at + 1) * total)
        pair[at] = rounded[rows]
        query[at] = (rest[rows, :width] * head_dim ** (-0.5)).astype(BF16)
        gate[at] = rest[rows, 2 * width :].astype(BF16)
        values = rest[rows, width : 2 * width]
        swapped = []
        for start in range(0, total, 2 * half):
            swapped += [values[start + half : start + 2 * half], values[start : start + half]]
        value[at] = jnp.where(odd_lane, jnp.concatenate(swapped, axis=0), values).astype(BF16)
        lines = lax.dot_general(w_key[...], normed[rows], NT, preferred_element_type=F32)
        for start in range(0, total, 2 * half):
            block = lines[:, start : start + 2 * half]
            key[at, :, start : start + 2 * half] = jnp.where(odd_row, pltpu.roll(block, half, 1), block).astype(BF16)


def attention_kernel(heads, n_cols, splits, tokens, key, query, value, gate, pair, w_out, *refs):
    n_rows, count = len(splits), sum(splits)
    bias = [refs[sum(splits[:step]) : sum(splits[: step + 1])] for step in range(n_rows)]
    updated, mirrored, biased, result = refs[count], refs[count + 1 : -2], refs[-2], refs[-1]
    width, total = key.shape[1:]
    cols_dev = bias[0][0].shape[2]
    rows_dev = updated.shape[2]
    halves = n_rows // n_cols
    head_dim = width // heads
    row_at, col_at = lax.axis_index("row"), lax.axis_index("col")
    lane = lax.broadcasted_iota(jnp.int32, (1, width), 1)

    @pl.when(pl.program_id(0) == 0)
    def _():
        from_own = (lane < rows_dev) != (row_at % 2 == 1)
        for step in range(0, n_rows, 2):
            spot = (row_at ^ step) // 2
            start = pl.multiple_of(spot * cols_dev, cols_dev)
            mask = (tokens[3:4, pl.ds(start, cols_dev)].astype(F32) - 1.0) * 30000.0
            for duo in range(heads // 2):
                masks = [mask, jnp.concatenate([mask[:, rows_dev:], mask[:, :rows_dev]], axis=1)]
                for block in range(n_cols):
                    piece, spot_in = divmod(block, n_cols // splits[step])
                    tiles = bias[step][piece][spot_in, duo], bias[step + 1][piece][spot_in, duo]
                    rows = pl.ds(pl.multiple_of((col_at ^ block) * cols_dev, cols_dev), cols_dev)
                    biased[spot, 2 * duo, rows] = jnp.where(from_own, tiles[0], tiles[1]) + masks[0]
                    biased[spot, 2 * duo + 1, rows] = jnp.where(from_own, tiles[1], tiles[0]) + masks[1]

    own_key, own_query = key[0], query[0]
    own_value = jnp.concatenate([value[0], jnp.ones((total, width), BF16)], axis=1)
    blocks = [jnp.zeros((cols_dev, width), F32)] * (total // cols_dev)
    wholes = list(blocks)
    for head in range(heads):
        inside = lane // head_dim == head
        for at in range(len(blocks)):
            rows = slice(at * cols_dev, (at + 1) * cols_dev)
            own = jnp.where(inside, own_query[rows], jnp.zeros((), BF16))
            score = jnp.dot(own, own_key, preferred_element_type=F32)
            score = score + jnp.concatenate([biased[spot, head, rows] for spot in range(biased.shape[0])], axis=1)
            highest = jnp.max(score, axis=1, keepdims=True)
            raised = jnp.exp(score - highest).astype(BF16)
            summed = jnp.dot(raised, own_value, preferred_element_type=F32)
            blocks[at] = jnp.where(inside, summed[:, :width], blocks[at])
            wholes[at] = jnp.where(inside, summed[:, width:], wholes[at])
    attended = jnp.concatenate(blocks, axis=0) / jnp.concatenate(wholes, axis=0)
    gated = (jax.nn.sigmoid(gate[0].astype(F32)) * attended).astype(BF16)
    update = jnp.dot(gated, w_out[...], preferred_element_type=F32)
    result[...] = (pair[0].astype(F32) + update).astype(BF16).reshape(result.shape)
    updated[:, 0] = result[...]
    for shift in range(n_cols):
        block = (row_at % n_cols) ^ shift
        mirrored[shift][:, 0] = result[pl.ds(block * halves, halves)]


def logits_kernel(n_cols, parts, *refs):
    rounds = len(parts)
    own = refs[1 : 1 + rounds]
    mirrored = refs[1 + rounds : 1 + rounds + rounds * n_cols]
    w_both, logits, wide = refs[1 + rounds + rounds * n_cols :]
    n_rows, _, rows_dev, width = own[0].shape
    halves = n_rows // n_cols
    cols_dev = halves * rows_dev
    slab = sum(parts)
    pitch = wide.shape[0] // cols_dev
    at_shift = pl.program_id(0)

    @pl.when(at_shift == 0)
    def _():
        for row in range(n_rows):
            for step in range(rounds):
                for at in range(parts[step]):
                    first = (row * slab + sum(parts[:step]) + at) * pitch
                    wide[first : first + rows_dev, :] = own[step][row, at].astype(F32)

    first = refs[0][at_shift] * slab
    for shift in range(n_cols):

        @pl.when(at_shift == shift)
        def _():
            for step in range(rounds):
                done = sum(parts[:step])
                mine, other = [], []
                for at in range(parts[step]):
                    mine.append(wide[pl.ds(first + done + at, cols_dev, stride=pitch), :])
                    other += [mirrored[step * n_cols + shift][half, at] for half in range(halves)]
                mine, other = jnp.concatenate(mine, axis=0), jnp.concatenate(other, axis=0)
                short = mine.astype(BF16)
                summed = mine + other.astype(F32)
                both = jnp.concatenate([normalise(mine, [short]), normalise(summed, [short, other])], axis=1)
                found = jnp.dot(both, w_both[...], preferred_element_type=F32)
                logits[done : done + parts[step]] = found.reshape(parts[step], cols_dev, found.shape[1])


def swap_over(array, axis, step, count):
    return lax.ppermute(array, axis, [(at, at ^ step) for at in range(count)])


def per_device(z_trunk, coords, token_mask, w_dist, w_attn, w_bias, w_out, w_pae, w_pde):
    rows_dev, cols_dev, width = z_trunk.shape
    n_rows, n_cols = lax.axis_size("row"), lax.axis_size("col")
    total = rows_dev * n_rows
    slab = rows_dev // n_cols
    halves = cols_dev // rows_dev
    heads = w_bias.shape[1]
    head_dim = width // heads
    classes = w_dist.shape[0]
    row_at, col_at = lax.axis_index("row"), lax.axis_index("col")
    params = pltpu.CompilerParams(vmem_limit_bytes=VMEM_LIMIT)
    vmem = pl.BlockSpec(memory_space=pltpu.VMEM)
    smem = pl.BlockSpec(memory_space=pltpu.SMEM)
    once = pl.Buffered(1)
    whole = lambda array: pl.BlockSpec(array.shape, lambda *at: (0,) * array.ndim, pipeline_mode=once)

    edges = (27.0 + 4.0 * jnp.arange(classes - 1, dtype=F32)) ** 2
    low = jnp.concatenate([jnp.full((1,), -1.0, F32), edges, jnp.full((width - classes,), 1e9, F32)])[None]
    high = jnp.concatenate([edges, jnp.full((width - classes + 1,), 1e9, F32)])[None]
    w_dist_full = jnp.pad(w_dist, ((0, width - classes), (0, 0)))
    w_bias_t = jnp.pad(w_bias.T, ((0, 16 - heads), (0, 0)))

    tokens = jnp.concatenate([coords, token_mask[None, :]], axis=0)
    copies = jnp.broadcast_to(tokens[None], (n_rows * n_cols,) + tokens.shape)
    tokens = lax.all_to_all(copies, AXES, split_axis=0, concat_axis=0, tiled=True)
    tokens = tokens.transpose(1, 0, 2).reshape(4, total)
    z_parts = z_trunk.reshape(rows_dev, n_rows, slab, width).swapaxes(0, 1)
    early = (z_parts, w_dist_full, w_bias_t, low, high)
    z_parts, w_dist_full, w_bias_t, low, high = lax.optimization_barrier(early)
    z_cols = lax.all_to_all(z_parts, "row", split_axis=0, concat_axis=0, tiled=True)
    z_cols = z_cols.reshape(total, slab, width)

    bias = pl.pallas_call(
        functools.partial(bias_kernel, 32),
        out_shape=jax.ShapeDtypeStruct((heads // 2, cols_dev, 2 * rows_dev), F32),
        in_specs=[smem] + [vmem] * 6,
        out_specs=vmem,
        scratch_shapes=[pltpu.VMEM((heads, rows_dev, cols_dev), F32), pltpu.VMEM((3, cols_dev, width), F32)],
        compiler_params=params,
        cost_estimate=pl.CostEstimate(flops=rows_dev * cols_dev * width * 300, bytes_accessed=1 << 22, transcendentals=0),
        name="bias_kernel",
    )(tokens, tokens, low, high, z_trunk, w_dist_full, w_bias_t)

    plane = jnp.stack([bias] + [swap_over(bias, "col", step, n_cols) for step in range(1, n_cols)])
    held = {0: [plane]}
    for step in range(2, n_rows, 2):
        if step & (step - 1) == 0:
            held[step] = [swap_over(plane, "row", step, n_rows)]

    w_key = w_attn[:, width : 2 * width].T
    w_rest = jnp.concatenate([w_attn[:, :width], w_attn[:, 2 * width :]], axis=1)
    rounds = 2
    parts = tuple((slab + rounds - 1 - step) // rounds for step in range(rounds))

    def project(step):
        done, part = sum(parts[:step]), parts[step]
        batch = min(2, part)
        spread_rows = -(-(done + part) // 8) * 8 - done // 8 * 8
        by_rows = pl.BlockSpec((batch, total, width), lambda j: (j, 0, 0))
        by_lanes = pl.BlockSpec((batch, width, total), lambda j: (j, 0, 0))
        rows_shape = jax.ShapeDtypeStruct((part, total, width), BF16)
        lanes_shape = jax.ShapeDtypeStruct((part, width, total), BF16)
        return pl.pallas_call(
            functools.partial(project_kernel, head_dim, batch, done, part),
            out_shape=(rows_shape, lanes_shape, rows_shape, rows_shape, rows_shape),
            grid=(part // batch,),
            in_specs=[smem, whole(tokens), vmem, vmem, whole(z_cols), vmem, vmem, vmem],
            out_specs=(by_rows, by_lanes, by_rows, by_rows, by_rows),
            scratch_shapes=[pltpu.VMEM(((total + 1) * spread_rows, width), F32), pltpu.VMEM((3, total, width), F32)],
            compiler_params=params,
            cost_estimate=pl.CostEstimate(
                flops=total * part * width * 2000, bytes_accessed=1 << 23, transcendentals=0
            ),
            name="project_kernel",
        )(tokens, tokens, low, high, z_cols, w_dist_full, w_key, w_rest)

    projected = [project(0)]
    held, projected = lax.optimization_barrier((held, projected))
    for step in range(2, n_rows, 2):
        one = step & -step
        if step != one:
            cut = n_cols // 2
            first, second = held[step ^ one], held[one]
            first = first[0] if len(first) == 2 else first[0][:cut]
            second = second[1] if len(second) == 2 else second[0][cut:]
            held[step] = [swap_over(first, "row", one, n_rows), swap_over(second, "row", step ^ one, n_rows)]
    projected.append(project(1))
    passed_on = {step: held[step] for step in range(2, n_rows, 2) if step & (step - 1)}
    passed_on, projected = lax.optimization_barrier((passed_on, projected))
    held |= passed_on
    for step in range(0, n_rows, 2):
        held[step + 1] = [swap_over(tile, "row", 1, n_rows) for tile in held[step]]
    splits = tuple(len(held[step]) for step in range(n_rows))
    tiles = [tile for step in range(n_rows) for tile in held[step]]

    own, mirrored = [], []
    for step, part in enumerate(parts):
        pair, key, query, value, gate = projected[step]
        rows_spec = pl.BlockSpec((1, total, width), lambda j: (j, 0, 0))
        lanes_spec = pl.BlockSpec((1, width, total), lambda j: (j, 0, 0))
        out_spec = lambda count: pl.BlockSpec((count, 1, rows_dev, width), lambda j: (0, j, 0, 0))
        out_shape = lambda count: jax.ShapeDtypeStruct((count, part, rows_dev, width), BF16)
        updated, *turned = pl.pallas_call(
            functools.partial(attention_kernel, heads, n_cols, splits),
            out_shape=(out_shape(n_rows),) + (out_shape(halves),) * n_cols,
            grid=(part,),
            in_specs=[whole(tokens), lanes_spec, rows_spec, rows_spec, rows_spec, rows_spec, whole(w_out)]
            + [whole(tile) for tile in tiles],
            out_specs=(out_spec(n_rows),) + (out_spec(halves),) * n_cols,
            scratch_shapes=[
                pltpu.VMEM((total // cols_dev, heads, total, cols_dev), F32),
                pltpu.VMEM((n_rows, rows_dev, width), BF16),
            ],
            compiler_params=params,
            cost_estimate=pl.CostEstimate(
                flops=4 * part * total * total * heads * 256,
                bytes_accessed=1 << 24,
                transcendentals=part * heads * total * total,
            ),
            name="attention_kernel",
        )(tokens, key, query, value, gate, pair, w_out, *tiles)
        if step:
            updated, turned, own, mirrored = lax.optimization_barrier((updated, turned, own, mirrored))
        own.append(lax.all_to_all(updated, "row", split_axis=0, concat_axis=0, tiled=True))
        for shift in range(n_cols):
            hops = []
            for r in range(n_rows):
                for c in range(n_cols):
                    to = (halves * c + r // n_cols) * n_cols + (r % n_cols ^ shift)
                    hops.append((r * n_cols + c, to))
            mirrored.append(lax.ppermute(turned[shift], AXES, hops))

    spots = jnp.stack([col_at ^ shift for shift in range(n_cols)]).astype(jnp.int32)
    bins = w_pae.shape[1]
    w_both = jnp.concatenate(
        [jnp.pad(w_pae, ((0, 0), (0, bins))), jnp.pad(w_pde, ((0, 0), (bins, 0)))], axis=0
    )
    return pl.pallas_call(
        functools.partial(logits_kernel, n_cols, parts),
        out_shape=jax.ShapeDtypeStruct((rows_dev, cols_dev, 2 * bins), F32),
        grid_spec=pltpu.PrefetchScalarGridSpec(
            num_scalar_prefetch=1,
            grid=(n_cols,),
            in_specs=[whole(array) for array in own + mirrored + [w_both]],
            out_specs=pl.BlockSpec((slab, cols_dev, 2 * bins), lambda b, at: (at[b], 0, 0)),
            scratch_shapes=[pltpu.VMEM(((cols_dev + 1) * (rows_dev + 8), width), F32)],
        ),
        compiler_params=params,
        name="logits_kernel",
    )(spots, *own, *mirrored, w_both)


def solution(mesh):
    in_specs = (
        P("row", "col", None),
        P(None, ("row", "col")),
        P(("row", "col")),
        P(),
        P(),
        P(),
        P(),
        P(),
        P(),
    )
    out_specs = P("row", "col", None)
    return jax.shard_map(
        per_device, mesh=mesh, in_specs=in_specs, out_specs=out_specs, check_vma=False
    )
```
